32 devices in a mesh: th: 4 (over x, core), tw: 8 (over z, y).
Axes of the slice: x: 2, y: 2, z: 4, core: 2. Of those that a mesh axis runs over, the one named last changes fastest.
Arguments:
- image: bfloat16 [256, 768, 384], P('th', 'tw'), may hold values from -6 to 6
- image_heights: int32 [3], replicated, may hold values from 1 to 192, as said below
- rate_log: float32 [2, 384, 32], replicated, may hold values from -1.5 to 1
- freq: float32 [2, 384, 32], replicated, may hold values from 0 to 3
- coef_re: float32 [2, 384, 32], replicated, may hold values from -0.18 to 0.18
- coef_im: float32 [2, 384, 32], replicated, may hold values from -0.18 to 0.18
- log_step: float32 [2, 384], replicated, may hold values from -3 to -0.5
- skip: float32 [384], replicated, may hold values from -3 to 3
- ln_gain: float32 [384], replicated, may hold values from 0.5 to 1.5
- ln_bias: float32 [384], replicated, may hold values from -1.8 to 1.8
- w_in: bfloat16 [384, 1536], replicated, may hold values from -0.3125 to 0.3125
- b_in: float32 [1536], replicated, may hold values from -1.8 to 1.8
- w_out: bfloat16 [1536, 384], replicated, may hold values from -0.15625 to 0.15625
- b_out: float32 [384], replicated, may hold values from -1.8 to 1.8
- layer_scale: float32 [384], replicated, may hold values from 0.5 to 2
- out_grad: bfloat16 [256, 768, 384], P('th', 'tw'), may hold values from -6 to 6
Outputs:
- output: bfloat16 [256, 768, 384], P('th', 'tw')
- image_grad: bfloat16 [256, 768, 384], P('th', 'tw')
- grad_rate_log: float32 [2, 384, 32], replicated
- grad_freq: float32 [2, 384, 32], replicated
- grad_coef_re: float32 [2, 384, 32], replicated
- grad_coef_im: float32 [2, 384, 32], replicated
- grad_log_step: float32 [2, 384], replicated
- grad_skip: float32 [384], replicated
- grad_ln_gain: float32 [384], replicated
- grad_ln_bias: float32 [384], replicated
- grad_w_in: float32 [384, 1536], replicated
- grad_b_in: float32 [1536], replicated
- grad_w_out: float32 [1536, 384], replicated
- grad_b_out: float32 [384], replicated
- grad_layer_scale: float32 [384], replicated
The draws below stay inside these ranges and needn't reach their ends.
Inputs may be any that keep to these rules, and one draw needn't show every extreme that they name: `image_heights`: 3 images stacked top to bottom, each as wide as the grid; the first and the last together have 64 rows, each at least one, and the middle one has exactly 192 rows.
All inputs are finite; a program needn't handle non-finite values.
Results may differ from the reference program's by a relative error of at most 0.005.
The reference program's roundings to bfloat16 on the way count: a program that leaves them out, or rounds other values in their place, can miss the bound.
Values may be sent and summed in bfloat16 or wider, within the bound.
No kernel may reach another device: no remote copies, remote signals or barrier semaphores. Data moves between devices by JAX's collectives and lax.ppermute only.
A program may use at most 384 MiB of HBM per device.

```python
import math
import jax
import jax.numpy as jnp
from jax import lax

C = 384
MLP = 1536
MODES = 32
KSIZE = 15
TH = 64
TW = 96
NH = 256
NW = 768
N_TH = 4
N_TW = 8


def draw_image_heights(key, part):
    first = jax.random.randint(jax.random.fold_in(key, 17), (), 1, TH, dtype=jnp.int32)
    middle = jnp.int32(NH - TH)
    return jnp.stack([first, middle, jnp.int32(TH) - first]).astype(jnp.int32)


def block_scale(key, shape, pieces, low, largest):
    loudness, own = 1.0, jax.random.fold_in(key, 6)
    for axis_at, blocks in pieces:
        heights = jnp.exp(jax.random.uniform(jax.random.fold_in(own, axis_at), (blocks,), jnp.float32, low / len(pieces), largest / len(pieces)))
        loudness = loudness * jnp.repeat(heights, shape[axis_at] // blocks).reshape([-1 if axis == axis_at else 1 for axis in range(len(shape))])
    return loudness


def normal_values(key, extent, deviation, bound, cuts=(), kind=jnp.bfloat16):
    entries = jax.random.normal(key, extent, jnp.float32) * deviation
    if len(cuts) > 0:
        entries = block_scale(key, extent, cuts, -0.22, 0.18) * entries
    return jnp.clip(entries, min=-bound, max=bound).astype(kind)


def setup_inputs(seed: int = 0) -> dict:
    streams_of = jax.random.split(jax.random.key(seed), 17)
    return {
        "image": normal_values(streams_of[0], (NH, NW, C), 1.0, 6.0, ((0, 4), (1, 8))),
        "image_heights": draw_image_heights(jax.random.fold_in(streams_of[16], 71), 0),
        "rate_log": jnp.clip(jax.random.uniform(streams_of[2], (2, C, MODES), jnp.float32, -1.5, 1.0), -1.5, 1.0),
        "freq": jnp.clip(jax.random.uniform(streams_of[3], (2, C, MODES), jnp.float32, 0.0, 3.0), 0.0, 3.0),
        "coef_re": normal_values(streams_of[4], (2, C, MODES), 0.03, 0.18, (), jnp.float32),
        "coef_im": normal_values(streams_of[5], (2, C, MODES), 0.03, 0.18, (), jnp.float32),
        "log_step": jnp.clip(jax.random.uniform(streams_of[6], (2, C), jnp.float32, -3.0, -0.5), -3.0, -0.5),
        "skip": normal_values(streams_of[7], (C,), 1.0, 3.0, (), jnp.float32),
        "ln_gain": jnp.clip(1.0 + 0.1 * jax.random.normal(streams_of[8], (C,), jnp.float32), 0.5, 1.5),
        "ln_bias": normal_values(streams_of[9], (C,), 0.3, 1.8, (), jnp.float32),
        "w_in": normal_values(streams_of[10], (C, MLP), C ** -0.5, 0.3125),
        "b_in": normal_values(streams_of[11], (MLP,), 0.3, 1.8, (), jnp.float32),
        "w_out": normal_values(streams_of[12], (MLP, C), MLP ** -0.5, 0.15625),
        "b_out": normal_values(streams_of[13], (C,), 0.3, 1.8, (), jnp.float32),
        "layer_scale": jnp.clip(jnp.exp(jax.random.uniform(streams_of[14], (C,), jnp.float32, math.log(0.5), math.log(2.0))), 0.5, 2.0),
        "out_grad": normal_values(streams_of[15], (NH, NW, C), 1.0, 6.0, ((0, 4), (1, 8))),
    }


@jax.custom_vjp
def low(v):
    return lax.optimization_barrier(v.astype(jnp.bfloat16)).astype(jnp.float32)

@jax.custom_vjp
def low_back(v):
    return v

def low_keep(v):
    return (low(v), None)

def low_pass(kept, grad):
    return (grad,)

def back_keep(v):
    return (v, None)

def back_low(kept, grad):
    return (low(grad),)
low.defvjp(low_keep, low_pass)
low_back.defvjp(back_keep, back_low)

def kernel_taps(rate_log, freq, coef_re, coef_im, log_step):
    step = jnp.exp(log_step)[:, None, :, None]
    offsets = jnp.arange(KSIZE, dtype=jnp.float32)[None, :, None, None]
    decay = jnp.exp(-jnp.exp(rate_log)[:, None] * step * offsets)
    phase = freq[:, None] * step * offsets
    terms = decay * (coef_re[:, None] * jnp.cos(phase) - coef_im[:, None] * jnp.sin(phase))
    return 2.0 * lax.optimization_barrier(jnp.sum(terms, axis=-1))

def normalize(mixed, gain, bias):
    mean = lax.optimization_barrier(jnp.mean(mixed, axis=-1, keepdims=True))
    centred = mixed - mean
    var = lax.optimization_barrier(jnp.mean(centred * centred, axis=-1, keepdims=True))
    return centred * lax.rsqrt(var + 1e-06) * gain + bias

def reference(image, image_heights, rate_log, freq, coef_re, coef_im, log_step, skip, ln_gain, ln_bias, w_in, b_in, w_out, b_out, layer_scale, out_grad):
    bounds = jnp.cumsum(image_heights).astype(jnp.int32)
    halo = KSIZE // 2
    high = lax.Precision.HIGHEST

    def forward(image_f, rate_log, freq, coef_re, coef_im, log_step, skip, ln_gain, ln_bias, w_in_f, b_in, w_out_f, b_out, layer_scale):
        taps = kernel_taps(rate_log, freq, coef_re, coef_im, log_step)
        padded = jnp.pad(image_f, ((halo, halo), (halo, halo), (0, 0)))

        def one_tile(index):
            tile_row = index // N_TW
            tile_col = index % N_TW
            start_row = (tile_row * TH).astype(jnp.int32)
            start_col = (tile_col * TW).astype(jnp.int32)
            ext = lax.dynamic_slice(padded, (start_row, start_col, jnp.int32(0)), (TH + 2 * halo, TW + 2 * halo, C))
            rows = start_row - halo + jnp.arange(TH + 2 * halo, dtype=jnp.int32)
            ident = lax.optimization_barrier(jnp.sum((rows[:, None] >= bounds[None, :]).astype(jnp.int32), axis=1))
            partial_value = jnp.zeros((TH, TW + 2 * halo, C), jnp.float32)
            for tap in range(KSIZE):
                same = (ident[halo:halo + TH] == ident[tap:tap + TH]).astype(jnp.float32)
                partial_value = partial_value + taps[0, tap][None, None, :] * same[:, None, None] * ext[tap:tap + TH]
            mixed = skip * ext[halo:halo + TH, halo:halo + TW]
            for tap in range(KSIZE):
                mixed = mixed + taps[1, tap][None, None, :] * partial_value[:, tap:tap + TW]
            mixed = low_back(mixed)
            normed = low(normalize(mixed, ln_gain, ln_bias)).reshape(TH * TW, C)
            pre = low_back(jnp.dot(normed, w_in_f, precision=high, preferred_element_type=jnp.float32) + b_in)
            act = low(jax.nn.gelu(pre, approximate=False))
            branch = low_back(jnp.dot(act, w_out_f, precision=high, preferred_element_type=jnp.float32) + b_out)
            centre = ext[halo:halo + TH, halo:halo + TW].reshape(TH * TW, C)
            return (centre + layer_scale * branch).reshape(TH, TW, C)
        tiles = lax.map(jax.checkpoint(one_tile), jnp.arange(N_TH * N_TW, dtype=jnp.int32))
        return tiles.reshape(N_TH, N_TW, TH, TW, C).transpose(0, 2, 1, 3, 4).reshape(NH, NW, C)
    inputs = (image.astype(jnp.float32), rate_log, freq, coef_re, coef_im, log_step, skip, ln_gain, ln_bias, w_in.astype(jnp.float32), b_in, w_out.astype(jnp.float32), b_out, layer_scale)
    result, pullback = jax.vjp(forward, *inputs)
    grads = pullback(out_grad.astype(jnp.float32))
    return (result.astype(jnp.bfloat16), grads[0].astype(jnp.bfloat16), grads[1], grads[2], grads[3], grads[4], grads[5], grads[6], grads[7], grads[8], grads[9], grads[10], grads[11], grads[12], grads[13])
```

```python
import functools

import jax
import jax.numpy as jnp
from jax import lax
from jax.experimental import pallas as pl
from jax.experimental.pallas import tpu as pltpu
from jax.sharding import PartitionSpec as P

KSIZE = 15
REACH = KSIZE // 2
EDGE = 8
LANES = 128
MIB = 2**20


def shift(block, axis, step):
    count = lax.axis_size(axis)
    pairs = [(i, i + step) for i in range(count) if 0 <= i + step < count]
    return lax.ppermute(block, axis, pairs)


def swap(block, axis, bit):
    count = lax.axis_size(axis)
    return lax.ppermute(block, axis, [(i, i ^ bit) for i in range(count)])


def halo(block):
    above = shift(block[-REACH:], "th", 1)
    below = shift(block[:REACH], "th", -1)
    tall_right = jnp.concatenate([above[:, -EDGE:], block[:, -EDGE:], below[:, -EDGE:]], axis=0)
    tall_left = jnp.concatenate([above[:, :EDGE], block[:, :EDGE], below[:, :EDGE]], axis=0)
    left = shift(tall_right, "tw", 1)
    right = shift(tall_left, "tw", -1)
    return above, below, left, right


def powers(rate, freq, log_step):
    step = jnp.exp(log_step)
    decay = jnp.exp(-jnp.exp(rate) * step)
    phase = freq * step
    return decay * jnp.cos(phase), decay * jnp.sin(phase), step


def taps_kernel(zr_ref, zi_ref, cr_ref, ci_ref, taps_ref):
    for d in range(2):
        zr, zi = zr_ref[d], zi_ref[d]
        cr, ci = cr_ref[d], ci_ref[d]
        ur, ui = jnp.ones_like(zr), jnp.zeros_like(zr)
        for m in range(KSIZE):
            taps_ref[d, m] = 2.0 * jnp.sum(cr * ur - ci * ui, axis=0)
            ur, ui = ur * zr - ui * zi, ur * zi + ui * zr
        taps_ref[d, KSIZE] = jnp.zeros_like(taps_ref[d, KSIZE])


def taps_grad_kernel(
    zr_ref, zi_ref, cr_ref, ci_ref, rate_ref, freq_ref, step_ref, g_ref,
    d_rate_ref, d_freq_ref, d_cr_ref, d_ci_ref, d_step_ref,
):
    for d in range(2):
        zr, zi = zr_ref[d], zi_ref[d]
        cr, ci = cr_ref[d], ci_ref[d]
        ur, ui = jnp.ones_like(zr), jnp.zeros_like(zr)
        su, sv = jnp.zeros_like(zr), jnp.zeros_like(zr)
        mu, mv = jnp.zeros_like(zr), jnp.zeros_like(zr)
        for m in range(KSIZE):
            g = 2.0 * g_ref[d, m][None, :]
            gu, gv = g * ur, g * ui
            su, sv = su + gu, sv + gv
            if m:
                mu, mv = mu + float(m) * gu, mv + float(m) * gv
            ur, ui = ur * zr - ui * zi, ur * zi + ui * zr
        step = step_ref[d][None, :]
        freq = freq_ref[d]
        d_freq = -step * (cr * mv + ci * mu)
        d_rate = -jnp.exp(rate_ref[d]) * step * (cr * mu - ci * mv)
        d_cr_ref[d] = su
        d_ci_ref[d] = -sv
        d_freq_ref[d] = d_freq
        d_rate_ref[d] = d_rate
        d_step_ref[d] = jnp.sum(d_rate + freq * d_freq, axis=0)


def load_tile(ext, centre, above, below, left, right, height, width):
    wide = ext.shape[1]
    at = 0 if left is None else EDGE
    full = height + 2 * REACH
    ext[full] = jnp.zeros(ext.shape[1:], jnp.float32)
    for i in range(REACH):
        ext[i, at : at + width] = above[i].astype(jnp.float32)
        ext[REACH + height + i, at : at + width] = below[i].astype(jnp.float32)

    def row(r, _):
        ext[r + REACH, at : at + width] = centre[r].astype(jnp.float32)
        return 0

    lax.fori_loop(0, height, row, 0)
    if left is not None:

        def sides(r, _):
            ext[r, 0:EDGE] = left[r].astype(jnp.float32)
            ext[r, EDGE + width : wide] = right[r].astype(jnp.float32)
            return 0

        lax.fori_loop(0, full, sides, 0)


def conv_kernel(
    source_ref, taps_ref, skip_ref, centre, above, below, left, right, mixed_ref, partial_ref, ext
):
    height, width = centre.shape[0], centre.shape[1]
    load_tile(ext, centre, above, below, left, right, height, width)
    rows = [taps_ref[0, i][None, :] for i in range(KSIZE)]
    cols = [taps_ref[1, j][None, :] for j in range(KSIZE)]
    skip = skip_ref[0][None, :]

    def row(r, _):
        total = rows[0] * ext[source_ref[r * KSIZE]]
        for i in range(1, KSIZE):
            total = total + rows[i] * ext[source_ref[r * KSIZE + i]]
        partial_ref[r] = total
        return 0

    lax.fori_loop(0, height, row, 0)

    def col(r, _):
        total = skip * ext[r + REACH, EDGE : EDGE + width]
        for j in range(KSIZE):
            total = total + cols[j] * partial_ref[r, 1 + j : 1 + j + width]
        mixed_ref[r] = total
        return 0

    lax.fori_loop(0, height, col, 0)


def conv_back_kernel(
    source_ref, taps_ref, skip_ref, partial_ref, grad_ref,
    centre, above, below, left, right, image, image_above, image_below,
    image_grad_ref, sums_ref, ext, image_ext, d_partial, col_sums, row_sums, skip_sums,
):
    height, width = centre.shape[0], centre.shape[1]
    full = height + 2 * REACH
    load_tile(ext, centre, above, below, left, right, height, width)
    load_tile(image_ext, image, image_above, image_below, None, None, height, width)
    rows = [taps_ref[0, i][None, :] for i in range(KSIZE)]
    cols = [taps_ref[1, j][None, :] for j in range(KSIZE)]
    skip = skip_ref[0][None, :]
    for sums in (col_sums, row_sums):
        sums[...] = jnp.zeros(sums.shape, jnp.float32)
    skip_sums[...] = jnp.zeros(skip_sums.shape, jnp.float32)
    d_partial[full] = jnp.zeros(d_partial.shape[1:], jnp.float32)

    def fold(v):
        return jnp.sum(v.reshape(width // 8, 8, v.shape[-1]), axis=0)

    def back_col(e, _):
        total = cols[0] * ext[e, KSIZE : KSIZE + width]
        for j in range(1, KSIZE):
            total = total + cols[j] * ext[e, KSIZE - j : KSIZE - j + width]
        d_partial[e] = total
        return 0

    lax.fori_loop(0, full, back_col, 0)

    def col_grad(r, _):
        d = ext[r + REACH, EDGE : EDGE + width]
        for j in range(KSIZE):
            col_sums[j] += fold(d * partial_ref[r, 1 + j : 1 + j + width])
        skip_sums[...] += fold(d * image_ext[r + REACH])
        return 0

    lax.fori_loop(0, height, col_grad, 0)

    def row_grad(r, _):
        d = d_partial[r + REACH]
        for i in range(KSIZE):
            row_sums[i] += fold(d * image_ext[source_ref[r * KSIZE + i]])
        return 0

    lax.fori_loop(0, height, row_grad, 0)

    def back_row(r, _):
        total = grad_ref[r].astype(jnp.float32) + skip * ext[r + REACH, EDGE : EDGE + width]
        for i in range(KSIZE):
            total = total + rows[i] * d_partial[source_ref[r * KSIZE + KSIZE - 1 - i]]
        image_grad_ref[r] = total.astype(jnp.bfloat16)
        return 0

    lax.fori_loop(0, height, back_row, 0)
    sums_ref[0:KSIZE] = jnp.sum(row_sums[...], axis=1)
    sums_ref[KSIZE : 2 * KSIZE] = jnp.sum(col_sums[...], axis=1)
    sums_ref[2 * KSIZE : 2 * KSIZE + 1] = jnp.sum(skip_sums[...], axis=0, keepdims=True)
    sums_ref[2 * KSIZE + 1 :] = jnp.zeros(
        (sums_ref.shape[0] - 2 * KSIZE - 1, sums_ref.shape[1]), jnp.float32
    )


def dot(a, b, dims=((1,), (0,))):
    return lax.dot_general(a, b, (dims, ((), ())), preferred_element_type=jnp.float32)


def feed_kernel(
    mixed_ref, image_ref, grad_ref, w_in_ref, w_out_t_ref, w_in_t_ref, w_out_ref,
    b_in_ref, vectors_ref,
    output_ref, d_mixed_ref, weights_ref, b_sums_ref, sums_ref,
    act_ref, d_pre_ref, total_ref,
):
    step = pl.program_id(0)
    chans, hidden = w_in_ref.shape
    piece = 512

    @pl.when(step == 0)
    def _():
        total_ref[...] = jnp.zeros(total_ref.shape, jnp.float32)
        b_sums_ref[...] = jnp.zeros(b_sums_ref.shape, jnp.float32)
        sums_ref[...] = jnp.zeros(sums_ref.shape, jnp.float32)

    gain, bias = vectors_ref[0:1], vectors_ref[1:2]
    b_out, scale = vectors_ref[2:3], vectors_ref[3:4]
    mixed = mixed_ref[...]
    mean = jnp.mean(mixed, axis=-1, keepdims=True)
    centred = mixed - mean
    var = jnp.mean(centred * centred, axis=-1, keepdims=True)
    inverse = lax.rsqrt(var + 1e-06)
    xhat = centred * inverse
    normed = (xhat * gain + bias).astype(jnp.bfloat16)
    grad = grad_ref[...].astype(jnp.float32)
    d_branch = (scale * grad).astype(jnp.bfloat16)
    normed_t = normed.T
    d_branch_t = d_branch.T
    ones = jnp.ones((8, normed.shape[0]), jnp.bfloat16)
    for k in range(0, hidden, piece):
        cut = slice(k, k + piece)
        pre = dot(normed, w_in_ref[:, cut]) + b_in_ref[:, cut]
        d_act = dot(d_branch, w_out_t_ref[:, cut])
        half = 0.5 + 0.5 * lax.erf(pre * 0.7071067811865476)
        bell = jnp.exp(pre * pre * -0.5) * 0.3989422804014327
        act = (pre * half).astype(jnp.bfloat16)
        d_pre = (d_act * (half + pre * bell)).astype(jnp.bfloat16)
        act_ref[:, cut] = act
        d_pre_ref[:, cut] = d_pre
        total_ref[0:chans, cut] += dot(normed_t, d_pre)
        total_ref[chans : 2 * chans, cut] += dot(d_branch_t, act)
        b_sums_ref[:, cut] += dot(ones, d_pre)
    branch = dot(act_ref[...], w_out_ref[...]) + b_out
    output_ref[...] = (image_ref[...].astype(jnp.float32) + scale * branch).astype(jnp.bfloat16)
    d_normed = dot(d_pre_ref[...], w_in_t_ref[...])

    def fold(v):
        return jnp.sum(v.reshape(v.shape[0] // 8, 8, v.shape[1]), axis=0)

    g = d_normed * gain
    g_mean = jnp.mean(g, axis=-1, keepdims=True)
    g_xhat = jnp.mean(g * xhat, axis=-1, keepdims=True)
    d_mixed_ref[...] = ((g - g_mean - xhat * g_xhat) * inverse).astype(jnp.bfloat16)
    sums_ref[0] += fold(d_normed * xhat)
    sums_ref[1] += fold(d_normed)
    sums_ref[2] += fold(d_branch.astype(jnp.float32))
    sums_ref[3] += fold(grad * branch)

    @pl.when(step == pl.num_programs(0) - 1)
    def _():
        weights_ref[...] = total_ref[...].astype(jnp.bfloat16)


def whole(shape):
    return pl.BlockSpec(shape, lambda *_: (0,) * len(shape))


def sum_over_mesh(part, steps):
    for axis, bit in steps:
        part = part + swap(part, axis, bit)
    return part


def mesh_steps():
    steps = []
    for axis in ("th", "tw"):
        bit = 1
        while bit < lax.axis_size(axis):
            steps.append((axis, bit))
            bit *= 2
    return steps


def scatter_gather(block, steps):
    places = []
    for axis, bit in steps:
        side = lax.rem(lax.axis_index(axis) // bit, 2)
        size = block.shape[0] // 2
        keep = lax.dynamic_slice_in_dim(block, side * size, size, 0)
        give = lax.dynamic_slice_in_dim(block, (1 - side) * size, size, 0)
        take = swap(give, axis, bit)
        block = (keep.astype(jnp.float32) + take.astype(jnp.float32)).astype(jnp.bfloat16)
        places.append((axis, bit, side))
    for axis, bit, side in reversed(places):
        other = swap(block, axis, bit)
        block = jnp.where(
            side == 0,
            jnp.concatenate([block, other], axis=0),
            jnp.concatenate([other, block], axis=0),
        )
    return block


def per_device(
    image, image_heights, rate_log, freq, coef_re, coef_im, log_step, skip, ln_gain, ln_bias,
    w_in, b_in, w_out, b_out, layer_scale, out_grad,
):
    height, width, chans = image.shape
    hidden = w_in.shape[1]
    pixels = height * width
    full = height + 2 * REACH
    wide = width + 2 * EDGE
    blocks = chans // LANES
    f32, bf16 = jnp.float32, jnp.bfloat16

    above, below, left, right = halo(image)

    first, second = image_heights[0], image_heights[0] + image_heights[1]
    start = lax.axis_index("th") * height

    def ident(r):
        return (r >= first).astype(jnp.int32) + (r >= second).astype(jnp.int32)

    row = jnp.arange(height, dtype=jnp.int32)[:, None]
    tap = jnp.arange(KSIZE, dtype=jnp.int32)[None, :]
    source = jnp.where(
        ident(start + row) == ident(start + row + tap - REACH), row + tap, full
    ).reshape(-1)

    rate_t, freq_t, cr_t, ci_t = (v.transpose(0, 2, 1) for v in (rate_log, freq, coef_re, coef_im))
    zr, zi, step = powers(rate_t, freq_t, log_step[:, None, :])
    step = step[:, 0]
    taps = pl.pallas_call(
        taps_kernel, out_shape=jax.ShapeDtypeStruct((2, KSIZE + 1, chans), f32)
    )(zr, zi, cr_t, ci_t)

    lane_block = lambda *lead: pl.BlockSpec((*lead, LANES), lambda c: (0,) * len(lead) + (c,))
    smem = pl.BlockSpec(memory_space=pltpu.SMEM)
    skip_row = skip[None, :]
    mixed, partial = pl.pallas_call(
        conv_kernel,
        grid=(blocks,),
        in_specs=[
            smem, lane_block(2, KSIZE + 1), lane_block(1), lane_block(height, width),
            lane_block(REACH, width), lane_block(REACH, width),
            lane_block(full, EDGE), lane_block(full, EDGE),
        ],
        out_specs=[lane_block(height, width), lane_block(height, wide)],
        out_shape=[
            jax.ShapeDtypeStruct((height, width, chans), f32),
            jax.ShapeDtypeStruct((height, wide, chans), f32),
        ],
        scratch_shapes=[pltpu.VMEM((full + 1, wide, LANES), f32)],
        compiler_params=pltpu.CompilerParams(vmem_limit_bytes=48 * MIB),
        cost_estimate=pl.CostEstimate(
            flops=60 * pixels * chans, bytes_accessed=12 * pixels * chans, transcendentals=0
        ),
        name="filter_forward",
    )(source, taps, skip_row, image, above, below, left, right)

    tile = 768
    pixel_block = pl.BlockSpec((tile, chans), lambda i: (i, 0))
    vectors = jnp.stack([ln_gain, ln_bias, b_out, layer_scale])
    output, d_mixed, weights, b_sums, sums = pl.pallas_call(
        feed_kernel,
        grid=(pixels // tile,),
        in_specs=[
            pixel_block, pixel_block, pixel_block,
            whole((chans, hidden)), whole((chans, hidden)), whole((hidden, chans)), whole((hidden, chans)),
            whole((1, hidden)), whole((4, chans)),
        ],
        out_specs=[
            pixel_block, pixel_block, whole((2 * chans, hidden)), whole((8, hidden)), whole((4, 8, chans)),
        ],
        out_shape=[
            jax.ShapeDtypeStruct((pixels, chans), bf16),
            jax.ShapeDtypeStruct((pixels, chans), bf16),
            jax.ShapeDtypeStruct((2 * chans, hidden), bf16),
            jax.ShapeDtypeStruct((8, hidden), f32),
            jax.ShapeDtypeStruct((4, 8, chans), f32),
        ],
        scratch_shapes=[
            pltpu.VMEM((tile, hidden), bf16),
            pltpu.VMEM((tile, hidden), bf16),
            pltpu.VMEM((2 * chans, hidden), f32),
        ],
        compiler_params=pltpu.CompilerParams(vmem_limit_bytes=60 * MIB),
        cost_estimate=pl.CostEstimate(
            flops=12 * pixels * chans * hidden, bytes_accessed=14 * pixels * chans, transcendentals=0
        ),
        name="feed_forward",
    )(
        mixed.reshape(pixels, chans), image.reshape(pixels, chans), out_grad.reshape(pixels, chans),
        w_in, w_out.T, w_in.T, w_out, b_in[None, :], vectors,
    )
    output = output.reshape(height, width, chans)
    d_mixed = d_mixed.reshape(height, width, chans)

    g_above, g_below, g_left, g_right = halo(d_mixed)
    n_sums = 2 * KSIZE + 2
    image_grad, tap_sums = pl.pallas_call(
        conv_back_kernel,
        grid=(blocks,),
        in_specs=[
            smem, lane_block(2, KSIZE + 1), lane_block(1), lane_block(height, wide), lane_block(height, width),
            lane_block(height, width), lane_block(REACH, width), lane_block(REACH, width),
            lane_block(full, EDGE), lane_block(full, EDGE),
            lane_block(height, width), lane_block(REACH, width), lane_block(REACH, width),
        ],
        out_specs=[lane_block(height, width), lane_block(n_sums)],
        out_shape=[
            jax.ShapeDtypeStruct((height, width, chans), bf16),
            jax.ShapeDtypeStruct((n_sums, chans), f32),
        ],
        scratch_shapes=[
            pltpu.VMEM((full + 1, wide, LANES), f32),
            pltpu.VMEM((full + 1, width, LANES), f32),
            pltpu.VMEM((full + 1, width, LANES), f32),
            pltpu.VMEM((KSIZE, 8, LANES), f32),
            pltpu.VMEM((KSIZE, 8, LANES), f32),
            pltpu.VMEM((8, LANES), f32),
        ],
        compiler_params=pltpu.CompilerParams(vmem_limit_bytes=60 * MIB),
        cost_estimate=pl.CostEstimate(
            flops=120 * pixels * chans, bytes_accessed=16 * pixels * chans, transcendentals=0
        ),
        name="filter_backward",
    )(
        source, taps, skip_row, partial, out_grad, d_mixed, g_above, g_below, g_left, g_right,
        image, above, below,
    )

    steps = mesh_steps()
    small = jnp.concatenate(
        [tap_sums, jnp.sum(sums, axis=1), b_sums[0].reshape(hidden // chans, chans)], axis=0
    )
    small = sum_over_mesh(small, steps)
    weights = scatter_gather(weights, steps).astype(f32)
    d_taps = small[: 2 * KSIZE].reshape(2, KSIZE, chans)
    d_skip = small[2 * KSIZE]
    d_gain, d_bias, d_bout, d_scale = (small[n_sums + i] for i in range(4))
    d_bin = small[n_sums + 4 :].reshape(hidden)

    mode_shape = jax.ShapeDtypeStruct(zr.shape, f32)
    g_rate, g_freq, g_re, g_im, g_step = pl.pallas_call(
        taps_grad_kernel,
        out_shape=[mode_shape] * 4 + [jax.ShapeDtypeStruct((2, chans), f32)],
    )(zr, zi, cr_t, ci_t, rate_t, freq_t, step, d_taps)
    g_rate, g_freq, g_re, g_im = (v.transpose(0, 2, 1) for v in (g_rate, g_freq, g_re, g_im))
    return (
        output, image_grad, g_rate, g_freq, g_re, g_im, g_step, d_skip, d_gain, d_bias,
        weights[:chans], d_bin, weights[chans:].T, d_bout, d_scale,
    )


def solution(mesh):
    tiled = P("th", "tw", None)
    return jax.shard_map(
        per_device,
        mesh=mesh,
        in_specs=(tiled,) + (P(),) * 14 + (tiled,),
        out_specs=(tiled, tiled) + (P(),) * 13,
        check_vma=False,
    )
```

```python
import jax
import jax.numpy as jnp
import ml_dtypes
import numpy as np
from jax import lax
from jax.experimental import pallas as pl
from jax.experimental.pallas import tpu as pltpu
from jax.sharding import PartitionSpec as P

KSIZE = 15
REACH = KSIZE // 2
EDGE = 8
LANES = 128
GROUP = 8
MIB = 2**20
F32, BF16 = jnp.float32, jnp.bfloat16


def swap(block, axis, bit):
    count = lax.axis_size(axis)
    return lax.ppermute(block, axis, [(i, i ^ bit) for i in range(count)])


def swap_across(block, axis):
    count = lax.axis_size(axis)
    pairs = [(i, i + 1) for i in range(1, count - 1, 2)]
    return lax.ppermute(block, axis, pairs + [(j, i) for i, j in pairs])


def tie(value, *others):
    return lax.optimization_barrier((value, *others))[0]


def halo_rows(block):
    place = lax.axis_index("th") % 2
    far = block.shape[0] - REACH
    near = swap(lax.dynamic_slice_in_dim(block, (1 - place) * far, REACH, 0), "th", 1)
    other = swap_across(lax.dynamic_slice_in_dim(block, place * far, REACH, 0), "th")
    return near, other


def halo_cols(block, near, other):
    place = lax.axis_index("tw") % 2
    far = block.shape[1] - EDGE

    def edge(at):
        return jnp.concatenate(
            [lax.dynamic_slice_in_dim(v, at * far, EDGE, 1) for v in (block, near, other)], axis=0
        )

    edges = edge(1 - place), edge(place)
    return swap(edges[0], "tw", 1), swap_across(edges[1], "tw"), edges


def two_parts(matrix):
    high = matrix.astype(ml_dtypes.bfloat16)
    low = (matrix - high.astype(np.float64)).astype(ml_dtypes.bfloat16)
    return np.concatenate([high, low], axis=1)


def transforms(width):
    size = width + 2 * EDGE
    half = size // 2
    place = np.concatenate([EDGE + np.arange(width), np.arange(EDGE), EDGE + width + np.arange(EDGE)])
    freq = np.arange(half)[:, None]

    def angle(n):
        return 2 * np.pi * ((freq * n[None, :]) % size) / size

    lower = -np.sin(angle(place))
    lower[0] = np.cos(np.pi * place)
    forward = np.concatenate([np.cos(angle(place)), lower])
    swapped = np.concatenate([forward[:, :width], forward[:, width + EDGE :], forward[:, width : width + EDGE]], axis=1)

    def back(n):
        real = 2 * np.cos(angle(n)) / size
        imag = -2 * np.sin(angle(n)) / size
        real[0] = 1 / size
        imag[0] = np.cos(np.pi * n) / size
        return np.concatenate([real, imag]).T

    ahead = back(1 + np.arange(width))
    behind = back(KSIZE + np.arange(width))
    lag = np.arange(KSIZE) - REACH
    real, high, imag = (np.zeros((KSIZE + 1, half)) for _ in range(3))
    real[:KSIZE] = (2 * np.cos(angle(lag)) / size).T
    high[:KSIZE] = real[:KSIZE]
    imag[:KSIZE] = (-2 * np.sin(angle(lag)) / size).T
    real[:KSIZE, 0] = 1 / size
    high[:KSIZE, 0] = np.cos(np.pi * lag) / size
    imag[:KSIZE, 0] = 0
    lags = np.concatenate([real, high, imag], axis=1).astype(np.float32)
    tap = np.arange(KSIZE + 1)
    real = np.cos(angle(tap))
    imag = np.sin(angle(tap))
    high = real.copy()
    high[0] = np.cos(np.pi * tap)
    response = np.concatenate([real, imag, high]).astype(np.float32)
    return (
        two_parts(forward), two_parts(swapped), two_parts(forward[:, :width]), two_parts(ahead), two_parts(behind),
        lags, response,
    )


def powers(rate, freq, log_step):
    step = jnp.exp(log_step)
    decay = jnp.exp(-jnp.exp(rate) * step)
    phase = freq * step
    return decay * jnp.cos(phase), decay * jnp.sin(phase), step


def dot(a, b, precision=None):
    return lax.dot_general(
        a, b, (((1,), (0,)), ((), ())), precision=precision, preferred_element_type=F32
    )


def taps_kernel(zr_ref, zi_ref, cr_ref, ci_ref, response_ref, taps_ref, factor_ref):
    half = factor_ref.shape[1]
    for d in range(2):
        zr, zi = zr_ref[d], zi_ref[d]
        cr, ci = cr_ref[d], ci_ref[d]
        ur, ui = jnp.ones_like(zr), jnp.zeros_like(zr)
        for m in range(KSIZE):
            taps_ref[d, m] = 2.0 * jnp.sum(cr * ur - ci * ui, axis=0)
            ur, ui = ur * zr - ui * zi, ur * zi + ui * zr
        taps_ref[d, KSIZE] = jnp.zeros_like(taps_ref[d, KSIZE])
    factor = dot(response_ref[...], taps_ref[1], lax.Precision.HIGHEST)
    for k in range(3):
        factor_ref[k] = factor[k * half : (k + 1) * half]


def taps_grad_kernel(
    zr_ref, zi_ref, cr_ref, ci_ref, rate_ref, freq_ref, step_ref, g_ref,
    d_rate_ref, d_freq_ref, d_cr_ref, d_ci_ref, d_step_ref,
):
    for d in range(2):
        zr, zi = zr_ref[d], zi_ref[d]
        cr, ci = cr_ref[d], ci_ref[d]
        ur, ui = jnp.ones_like(zr), jnp.zeros_like(zr)
        su, sv = jnp.zeros_like(zr), jnp.zeros_like(zr)
        mu, mv = jnp.zeros_like(zr), jnp.zeros_like(zr)
        for m in range(KSIZE):
            g = 2.0 * g_ref[d * (KSIZE + 1) + m][None, :]
            gu, gv = g * ur, g * ui
            su, sv = su + gu, sv + gv
            if m:
                mu, mv = mu + float(m) * gu, mv + float(m) * gv
            ur, ui = ur * zr - ui * zi, ur * zi + ui * zr
        step = step_ref[d][None, :]
        freq = freq_ref[d]
        d_freq = -step * (cr * mv + ci * mu)
        d_rate = -jnp.exp(rate_ref[d]) * step * (cr * mu - ci * mv)
        d_cr_ref[d] = su
        d_ci_ref[d] = -sv
        d_freq_ref[d] = d_freq
        d_rate_ref[d] = d_rate
        d_step_ref[d] = jnp.sum(d_rate + freq * d_freq, axis=0)


def load_rows(ext, source_ref, centre, near, other):
    height = centre.shape[0]
    ext[height + 2 * REACH] = jnp.zeros(ext.shape[1:], F32)
    for i in range(REACH):
        ext[source_ref[height * KSIZE] + i] = near[i].astype(F32)
        ext[source_ref[height * KSIZE + 1] + i] = other[i].astype(F32)

    def row(r, _):
        for k in range(4):
            ext[4 * r + k + REACH] = centre[4 * r + k].astype(F32)
        return 0

    lax.fori_loop(0, height // 4, row, 0)


def fold(v):
    return jnp.sum(v.reshape(v.shape[0] // 8, 8, v.shape[1]), axis=0)


def rows_kernel(source_ref, taps_ref, centre, near, other, partial_ref, ext):
    height = centre.shape[0]
    load_rows(ext, source_ref, centre, near, other)
    taps = [taps_ref[0, i][None, :] for i in range(KSIZE)]

    def row(r, _):
        for k in range(2):
            at = 2 * r + k
            total = taps[0] * ext[source_ref[at * KSIZE]]
            for i in range(1, KSIZE):
                total = total + taps[i] * ext[source_ref[at * KSIZE + i]]
            partial_ref[at] = total.astype(BF16)
        return 0

    lax.fori_loop(0, height // 2, row, 0)


def twice(v):
    return jnp.concatenate([v, v], axis=0)


def filtered(spectrum, factor, conjugate):
    half = factor[0].shape[0]
    real, imag = spectrum[:half], spectrum[half:]
    a, b, top = factor
    cross = b * imag
    across = b * real
    if conjugate:
        return jnp.concatenate([a * real + cross, top * imag - across], axis=0).astype(BF16)
    return jnp.concatenate([a * real - cross, top * imag + across], axis=0).astype(BF16)


def cols_kernel(
    source_ref, taps_ref, skip_ref, factor_ref, forward_ref, ahead_ref,
    partial_ref, image_ref, near, other,
    mixed_ref, spectrum_ref, sides, side_partial,
):
    step = pl.program_id(0)
    full = near.shape[0]
    height = full - 2 * REACH

    @pl.when(step == 0)
    def _():
        sides[full] = jnp.zeros(sides.shape[1:], F32)
        for part, at in ((near, 0), (other, EDGE)):
            for i in range(2 * REACH):
                base = source_ref[height * KSIZE + i // REACH] + i % REACH
                sides[base, at : at + EDGE] = part[height + i].astype(F32)

            def place(r, _):
                sides[r + REACH, at : at + EDGE] = part[r].astype(F32)
                return 0

            lax.fori_loop(0, height, place, 0)

        taps = [taps_ref[0, i][None, :] for i in range(KSIZE)]

        def row(r, _):
            total = taps[0] * sides[source_ref[r * KSIZE]]
            for i in range(1, KSIZE):
                total = total + taps[i] * sides[source_ref[r * KSIZE + i]]
            side_partial[r] = total.astype(BF16)
            return 0

        lax.fori_loop(0, height, row, 0)

    factor = [factor_ref[k] for k in range(3)]
    skip = skip_ref[...]
    for k in range(GROUP):
        line = jnp.concatenate([partial_ref[k], side_partial[step * GROUP + k]], axis=0)
        spectrum = dot(forward_ref[...], twice(line))
        spectrum_ref[k] = spectrum.astype(BF16)
        mixed = dot(ahead_ref[...], twice(filtered(spectrum, factor, False)))
        mixed_ref[k] = mixed + skip * image_ref[k].astype(F32)


def cols_grad_kernel(
    own_ref, lags_ref, d_mixed_ref, spectrum_ref, image_ref, sums_ref, totals, skip_total
):
    step = pl.program_id(0)
    half = totals.shape[1]

    @pl.when(step == 0)
    def _():
        totals[...] = jnp.zeros(totals.shape, F32)
        skip_total[...] = jnp.zeros(skip_total.shape, F32)

    for k in range(GROUP):
        d = d_mixed_ref[k]
        spectrum = dot(own_ref[...], twice(d))
        real, imag = spectrum[:half], spectrum[half:]
        other = spectrum_ref[k].astype(F32)
        other_real, other_imag = other[:half], other[half:]
        totals[0] += real * other_real
        totals[1] += imag * other_imag
        totals[2] += real * other_imag - imag * other_real
        skip_total[...] += fold(d.astype(F32) * image_ref[k].astype(F32))

    @pl.when(step == pl.num_programs(0) - 1)
    def _():
        both = jnp.concatenate([totals[0], totals[1], totals[2]], axis=0)
        sums_ref[...] = dot(lags_ref[...], both, lax.Precision.HIGHEST)
        sums_ref[KSIZE : KSIZE + 1] = jnp.sum(skip_total[...], axis=0, keepdims=True)


def cols_back_kernel(
    source_ref, factor_ref, forward_ref, behind_ref,
    centre, row_near, row_other, col_near, col_other, image, image_near, image_other,
    d_partial_ref, sums_ref, ext, d_partial, row_sums,
):
    height, width = centre.shape[0], centre.shape[1]
    load_rows(ext, source_ref, image, image_near, image_other)
    batch = 4
    factor = [jnp.concatenate([factor_ref[k]] * batch, axis=1) for k in range(3)]
    row_sums[...] = jnp.zeros(row_sums.shape, F32)

    def line(own, one, two):
        both = jnp.concatenate([one.astype(F32), two.astype(F32)], axis=0).astype(BF16)
        return jnp.concatenate([own, both], axis=0)

    def transformed(lines):
        spectrum = dot(forward_ref[...], twice(jnp.concatenate(lines, axis=1)))
        some = [f[:, : spectrum.shape[1]] for f in factor]
        return dot(behind_ref[...], twice(filtered(spectrum, some, True)))

    def group(g):
        found = transformed(
            [line(centre[r], col_near[r], col_other[r]) for r in (batch * g + k for k in range(batch))]
        )
        for k in range(batch):
            row = found[:, k * LANES : (k + 1) * LANES]
            d_partial[batch * g + k] = row
            d_partial_ref[REACH + batch * g + k] = row.astype(BF16)

    def grads(g):
        for k in range(batch):
            r = batch * g + k
            d = d_partial[r]
            for i in range(KSIZE):
                row_sums[i] += fold(d * ext[source_ref[r * KSIZE + i]])

    group(0)

    def both(g, _):
        group(g)
        grads(g - 1)
        return 0

    lax.fori_loop(1, height // batch, both, 0)
    grads(height // batch - 1)
    for n, rows in enumerate((row_near, row_other)):
        to = source_ref[height * KSIZE + n]
        base = height + n * REACH
        for at in range(0, REACH, batch):
            some = range(at, min(at + batch, REACH))
            found = transformed([line(rows[i], col_near[base + i], col_other[base + i]) for i in some])
            for k, i in enumerate(some):
                d_partial_ref[to + i] = found[:, k * LANES : (k + 1) * LANES].astype(BF16)
    sums_ref[0:KSIZE] = jnp.sum(row_sums[...], axis=1)
    sums_ref[KSIZE : KSIZE + 1] = jnp.zeros((1, LANES), F32)


def rows_back_kernel(source_ref, taps_ref, skip_ref, d_partial_ref, d_mixed_ref, grad_ref, *rest):
    image_grad_ref, ext = rest[-2:]
    step = pl.program_id(0)
    count = d_mixed_ref.shape[0]
    full = d_partial_ref.shape[0]

    @pl.when(step == 0)
    def _():
        ext[full] = jnp.zeros(ext.shape[1:], F32)

        def place(r, _):
            for k in range(2):
                ext[2 * r + k] = d_partial_ref[2 * r + k].astype(F32)
            return 0

        lax.fori_loop(0, full // 2, place, 0)

    taps = [taps_ref[0, i][None, :] for i in range(KSIZE)]
    skip = skip_ref[...]

    def row(r, _):
        for k in range(2):
            at = 2 * r + k
            total = grad_ref[at].astype(F32) + skip * d_mixed_ref[at].astype(F32)
            for i in range(KSIZE):
                place = (step * count + at) * KSIZE + KSIZE - 1 - i
                total = total + taps[i] * ext[source_ref[place]]
            image_grad_ref[at] = total.astype(BF16)
        return 0

    lax.fori_loop(0, count // 2, row, 0)


def feed_kernel(
    mixed_ref, image_ref, grad_ref, w_in_ref, w_out_t_ref, w_in_t_ref, w_out_ref,
    b_in_ref, vectors_ref,
    output_ref, d_mixed_ref, weights_ref, b_sums_ref, sums_ref,
    act_ref, d_pre_ref,
):
    step = pl.program_id(0)
    chans, hidden = w_in_ref.shape
    piece = 512

    @pl.when(step == 0)
    def _():
        weights_ref[...] = jnp.zeros(weights_ref.shape, F32)
        b_sums_ref[...] = jnp.zeros(b_sums_ref.shape, F32)
        sums_ref[...] = jnp.zeros(sums_ref.shape, F32)

    gain, bias = vectors_ref[0:1], vectors_ref[1:2]
    b_out, scale = vectors_ref[2:3], vectors_ref[3:4]
    mixed = mixed_ref[...]
    mean = jnp.mean(mixed, axis=-1, keepdims=True)
    centred = mixed - mean
    var = jnp.mean(centred * centred, axis=-1, keepdims=True)
    inverse = lax.rsqrt(var + 1e-06)
    xhat = centred * inverse
    normed = (xhat * gain + bias).astype(BF16)
    grad = grad_ref[...].astype(F32)
    d_branch = (scale * grad).astype(BF16)
    normed_t = normed.T
    d_branch_t = d_branch.T
    ones = jnp.ones((8, normed.shape[0]), BF16)
    for k in range(0, hidden, piece):
        cut = slice(k, k + piece)
        pre = dot(normed, w_in_ref[:, cut]) + b_in_ref[:, cut]
        d_act = dot(d_branch, w_out_t_ref[:, cut])
        half = 0.5 + 0.5 * lax.erf(pre * 0.7071067811865476)
        bell = jnp.exp(pre * pre * -0.5) * 0.3989422804014327
        act = (pre * half).astype(BF16)
        d_pre = (d_act * (half + pre * bell)).astype(BF16)
        act_ref[:, cut] = act
        d_pre_ref[:, cut] = d_pre
        weights_ref[0:chans, cut] += dot(normed_t, d_pre)
        weights_ref[chans : 2 * chans, cut] += dot(d_branch_t, act)
        b_sums_ref[:, cut] += dot(ones, d_pre)
    branch = dot(act_ref[...], w_out_ref[...]) + b_out
    output_ref[...] = (image_ref[...].astype(F32) + scale * branch).astype(BF16)
    d_normed = dot(d_pre_ref[...], w_in_t_ref[...])
    g = d_normed * gain
    g_mean = jnp.mean(g, axis=-1, keepdims=True)
    g_xhat = jnp.mean(g * xhat, axis=-1, keepdims=True)
    d_mixed_ref[...] = ((g - g_mean - xhat * g_xhat) * inverse).astype(BF16)
    sums_ref[0] += fold(d_normed * xhat)
    sums_ref[1] += fold(d_normed)
    sums_ref[2] += fold(d_branch.astype(F32))
    sums_ref[3] += fold(grad * branch)


def whole(shape):
    return pl.BlockSpec(shape, lambda *_: (0,) * len(shape))


def lane_block(*lead):
    return pl.BlockSpec((*lead, LANES), lambda c: (0,) * len(lead) + (c,))


def row_block(*rest):
    return pl.BlockSpec((GROUP, *rest), lambda r: (r,) + (0,) * len(rest))


SCALARS = pl.BlockSpec(memory_space=pltpu.SMEM)


def params():
    return pltpu.CompilerParams(vmem_limit_bytes=60 * MIB)


def cost(us):
    return pl.CostEstimate(flops=int(us * 1e8), bytes_accessed=int(us * 1e5), transcendentals=0)


def mesh_steps():
    def bits(axis):
        return [(axis, 1 << k) for k in range(lax.axis_size(axis).bit_length() - 1)]

    (core, *high), low = bits("th"), bits("tw")
    mixed = [step for pair in zip(high, low) for step in pair]
    return [core] + mixed + high[len(low) :] + low[len(high) :]


def swap_two(block, first, second):
    if first[0] == second[0]:
        return swap(block, first[0], first[1] + second[1])
    bits = dict([first, second])
    high, low = lax.axis_size("th"), lax.axis_size("tw")
    pairs = [
        (i * low + j, (i ^ bits["th"]) * low + (j ^ bits["tw"])) for i in range(high) for j in range(low)
    ]
    return lax.ppermute(block, ("th", "tw"), pairs)


def place_in(steps):
    place = 0
    for n, (axis, bit) in enumerate(steps):
        place = place + lax.rem(lax.axis_index(axis) // bit, 2) * (1 << n)
    return place


def exchanges(steps):
    if len(steps) == 1:
        return [lambda v: swap(v, *steps[0])]
    return [lambda v: swap(v, *steps[0]), lambda v: swap(v, *steps[1]), lambda v: swap_two(v, *steps)]


def scatter(block, steps, kind, beside):
    place = place_in(steps)
    count = 1 << len(steps)
    size = block.shape[0] // count
    total = lax.dynamic_slice_in_dim(block, place * size, size, 0)
    gives = [
        lax.dynamic_slice_in_dim(block, (place ^ k) * size, size, 0).astype(kind) for k in range(1, count)
    ]
    takes = [send(give) for send, give in zip(exchanges(steps), gives)]
    done = beside(gives)
    for take in takes:
        total = total + tie(take, *done).astype(F32)
    return total


def gather(block, steps, beside):
    place = place_in(steps)
    takes = [send(block) for send in exchanges(steps)]
    done = beside([block])
    parts = [block] + [tie(take, *done) for take in takes]
    rows = []
    for q in range(len(parts)):
        found = parts[-1]
        for k in range(len(parts) - 1):
            found = jnp.where((place ^ q) == k, parts[k], found)
        rows.append(found)
    return jnp.concatenate(rows, axis=0)


def finish_kernel(side_ref, own_ref, other_ref, w_in_ref, w_out_ref):
    side = side_ref[0]

    @pl.when(side == 0)
    def _():
        w_in_ref[...] = own_ref[...].astype(F32)
        w_out_ref[...] = other_ref[...].astype(F32).T

    @pl.when(side == 1)
    def _():
        w_in_ref[...] = other_ref[...].astype(F32)
        w_out_ref[...] = own_ref[...].astype(F32).T


def per_device(
    image, image_heights, rate_log, freq, coef_re, coef_im, log_step, skip, ln_gain, ln_bias,
    w_in, b_in, w_out, b_out, layer_scale, out_grad,
):
    height, width, chans = image.shape
    hidden = w_in.shape[1]
    pixels = height * width
    full = height + 2 * REACH
    size = width + 2 * EDGE
    half = size // 2
    blocks = chans // LANES
    groups = height // GROUP
    straight, swapped, own, ahead, behind, lags, response = transforms(width)
    forward = jnp.where(lax.axis_index("tw") % 2 == 1, straight, swapped)

    row_near, row_other = halo_rows(image)
    col_near, col_other, _ = halo_cols(image, row_near, row_other)

    first, second = image_heights[0], image_heights[0] + image_heights[1]
    start = lax.axis_index("th") * height

    def ident(r):
        return (r >= first).astype(jnp.int32) + (r >= second).astype(jnp.int32)

    row = jnp.arange(height, dtype=jnp.int32)[:, None]
    tap = jnp.arange(KSIZE, dtype=jnp.int32)[None, :]
    source = jnp.where(
        ident(start + row) == ident(start + row + tap - REACH), row + tap, full
    ).reshape(-1)
    base = jnp.where(jnp.arange(2) == lax.axis_index("th") % 2, REACH + height, 0)
    source = jnp.concatenate([source, base.astype(jnp.int32)])

    rate_t, freq_t, cr_t, ci_t = (v.transpose(0, 2, 1) for v in (rate_log, freq, coef_re, coef_im))
    zr, zi, step = powers(rate_t, freq_t, log_step[:, None, :])
    step = step[:, 0]
    taps, factor = pl.pallas_call(
        taps_kernel,
        out_shape=[
            jax.ShapeDtypeStruct((2, KSIZE + 1, chans), F32),
            jax.ShapeDtypeStruct((3, half, chans), F32),
        ],
        name="taps",
    )(zr, zi, cr_t, ci_t, response)

    skip_row = skip[None, :]
    tile_shape = (height, width, chans)
    partial = pl.pallas_call(
        rows_kernel,
        grid=(blocks,),
        in_specs=[
            SCALARS, lane_block(2, KSIZE + 1), lane_block(height, width),
            lane_block(REACH, width), lane_block(REACH, width),
        ],
        out_specs=lane_block(height, width),
        out_shape=jax.ShapeDtypeStruct(tile_shape, BF16),
        scratch_shapes=[pltpu.VMEM((full + 1, width, LANES), F32)],
        compiler_params=params(),
        cost_estimate=cost(14),
        name="rows_forward",
    )(source, taps, image, row_near, row_other)

    mixed, spectrum = pl.pallas_call(
        cols_kernel,
        grid=(groups,),
        in_specs=[
            SCALARS, whole((2, KSIZE + 1, chans)), whole((1, chans)), whole((3, half, chans)),
            whole((size, 2 * size)), whole((width, 2 * size)),
            row_block(width, chans), row_block(width, chans),
            whole((full, EDGE, chans)), whole((full, EDGE, chans)),
        ],
        out_specs=[row_block(width, chans), row_block(size, chans)],
        out_shape=[
            jax.ShapeDtypeStruct(tile_shape, F32),
            jax.ShapeDtypeStruct((height, size, chans), BF16),
        ],
        scratch_shapes=[
            pltpu.VMEM((full + 1, 2 * EDGE, chans), F32),
            pltpu.VMEM((height, 2 * EDGE, chans), BF16),
        ],
        compiler_params=params(),
        cost_estimate=cost(14),
        name="cols_forward",
    )(
        source, taps, skip_row, factor, forward, ahead, partial, image,
        col_near, col_other,
    )

    tile = 768
    pixel_block = pl.BlockSpec((tile, chans), lambda i: (i, 0))
    vectors = jnp.stack([ln_gain, ln_bias, b_out, layer_scale])
    output, d_mixed, weights, b_sums, sums = pl.pallas_call(
        feed_kernel,
        grid=(pixels // tile,),
        in_specs=[
            pixel_block, pixel_block, pixel_block,
            whole((chans, hidden)), whole((chans, hidden)), whole((hidden, chans)), whole((hidden, chans)),
            whole((1, hidden)), whole((4, chans)),
        ],
        out_specs=[
            pixel_block, pixel_block, whole((2 * chans, hidden)), whole((8, hidden)), whole((4, 8, chans)),
        ],
        out_shape=[
            jax.ShapeDtypeStruct((pixels, chans), BF16),
            jax.ShapeDtypeStruct((pixels, chans), BF16),
            jax.ShapeDtypeStruct((2 * chans, hidden), F32),
            jax.ShapeDtypeStruct((8, hidden), F32),
            jax.ShapeDtypeStruct((4, 8, chans), F32),
        ],
        scratch_shapes=[pltpu.VMEM((tile, hidden), BF16), pltpu.VMEM((tile, hidden), BF16)],
        compiler_params=params(),
        cost_estimate=cost(70),
        name="feed_forward",
    )(
        mixed.reshape(pixels, chans), image.reshape(pixels, chans), out_grad.reshape(pixels, chans),
        w_in, w_out.T, w_in.T, w_out, b_in[None, :], vectors,
    )
    output = output.reshape(tile_shape)
    d_mixed = d_mixed.reshape(tile_shape)

    grad_row_near, grad_row_other = halo_rows(d_mixed)
    grad_col_near, grad_col_other, edges = halo_cols(d_mixed, grad_row_near, grad_row_other)

    core, *others = mesh_steps()
    phases = [others[k : k + 2] for k in range(0, len(others), 2)]
    found = []

    def cols_grad(sent):
        found.append(
            pl.pallas_call(
                cols_grad_kernel,
                grid=(groups,),
                in_specs=[
                    whole((size, 2 * width)), whole((KSIZE + 1, 3 * half)),
                    row_block(width, chans), row_block(size, chans), row_block(width, chans),
                ],
                out_specs=whole((KSIZE + 1, chans)),
                out_shape=jax.ShapeDtypeStruct((KSIZE + 1, chans), F32),
                scratch_shapes=[pltpu.VMEM((3, half, chans), F32), pltpu.VMEM((8, chans), F32)],
                compiler_params=params(),
                cost_estimate=cost(8),
                name="cols_grad",
            )(own, lags, tie(d_mixed, *sent, *edges), spectrum, image)
        )
        return []

    weights = scatter(weights, [core], F32, cols_grad)
    (col_sums,) = found

    def cols_back(sent):
        both = pl.pallas_call(
            cols_back_kernel,
            grid=(blocks,),
            in_specs=[
                SCALARS, lane_block(3, half), whole((size, 2 * size)), whole((width, 2 * size)),
                lane_block(height, width), lane_block(REACH, width), lane_block(REACH, width),
                lane_block(full, EDGE), lane_block(full, EDGE),
                lane_block(height, width), lane_block(REACH, width), lane_block(REACH, width),
            ],
            out_specs=[lane_block(full, width), lane_block(KSIZE + 1)],
            out_shape=[
                jax.ShapeDtypeStruct((full, width, chans), BF16),
                jax.ShapeDtypeStruct((KSIZE + 1, chans), F32),
            ],
            scratch_shapes=[
                pltpu.VMEM((full + 1, width, LANES), F32),
                pltpu.VMEM((height, width, LANES), F32),
                pltpu.VMEM((KSIZE, 8, LANES), F32),
            ],
            compiler_params=params(),
            cost_estimate=cost(20),
            name="cols_back",
        )(
            source, factor, forward, behind, tie(d_mixed, *sent), grad_row_near, grad_row_other,
            grad_col_near, grad_col_other, image, row_near, row_other,
        )
        found.extend(both)
        return both

    weights = scatter(weights, phases[0], BF16, cols_back)
    _, d_partial, row_sums = found

    small = jnp.concatenate(
        [row_sums, col_sums, jnp.sum(sums, axis=1), b_sums[0].reshape(hidden // chans, chans)], axis=0
    )

    def rows_back(block, before, *waits):
        at = pl.BlockSpec((height // 4, width, LANES), lambda r: (r, 0, block))
        lanes = lambda *lead: pl.BlockSpec((*lead, LANES), lambda r: (0,) * len(lead) + (block,))
        return pl.pallas_call(
            rows_back_kernel,
            grid=(4,),
            in_specs=[
                SCALARS, lanes(2, KSIZE + 1), lanes(1), lanes(full, width), at, at,
                *([] if before is None else [pl.BlockSpec(memory_space=pl.ANY)]),
            ],
            out_specs=at,
            out_shape=jax.ShapeDtypeStruct(tile_shape, BF16),
            scratch_shapes=[pltpu.VMEM((full + 1, width, LANES), F32)],
            compiler_params=params(),
            cost_estimate=cost(6),
            input_output_aliases={} if before is None else {6: 0},
            name="rows_back",
        )(
            source, taps, tie(skip_row, *waits), d_partial, d_mixed, out_grad,
            *([] if before is None else [before]),
        )

    small = small + swap(small, *core)
    waiting = list(phases)

    def beside(block, before):
        def work(sent):
            nonlocal small
            takes = []
            if waiting:
                takes = [send(small) for send in exchanges(waiting.pop(0))]
            some = rows_back(block, before, *sent, small)
            for take in takes:
                small = small + tie(take, some)
            found.append(some)
            return [some]

        return work

    for n, later in enumerate(phases[1:]):
        weights = scatter(weights, later, F32, beside(0, None) if n == 0 else lambda _: [])
    weights = weights.astype(BF16)
    for n, later in enumerate(reversed(phases[1:])):
        weights = gather(weights, later, beside(1, found[-1]) if n == 0 else lambda _: [])
    for later in waiting:
        small = sum([send(small) for send in exchanges(later)], small)
    waiting.clear()
    weights = gather(tie(weights, small), phases[0], beside(2, found[-1]))
    image_grad = found[-1]
    cut = hidden // 4
    half_block = pl.BlockSpec((chans, cut), lambda k: (0, k))
    d_win, d_wout = pl.pallas_call(
        finish_kernel,
        grid=(4,),
        in_specs=[SCALARS, half_block, half_block],
        out_specs=[half_block, pl.BlockSpec((cut, chans), lambda k: (k, 0))],
        out_shape=[
            jax.ShapeDtypeStruct((chans, hidden), F32),
            jax.ShapeDtypeStruct((hidden, chans), F32),
        ],
        compiler_params=params(),
        cost_estimate=cost(3),
        name="weight_grads",
    )(place_in([core])[None], weights, swap(weights, *core))
    d_skip = small[2 * KSIZE + 1]
    n_sums = 2 * KSIZE + 2
    d_gain, d_bias, d_bout, d_scale = (small[n_sums + i] for i in range(4))
    d_bin = small[n_sums + 4 :].reshape(hidden)

    mode_shape = jax.ShapeDtypeStruct(zr.shape, F32)
    g_rate, g_freq, g_re, g_im, g_step = pl.pallas_call(
        taps_grad_kernel,
        out_shape=[mode_shape] * 4 + [jax.ShapeDtypeStruct((2, chans), F32)],
        name="taps_grad",
    )(zr, zi, cr_t, ci_t, rate_t, freq_t, step, small[:n_sums])
    g_rate, g_freq, g_re, g_im = (v.transpose(0, 2, 1) for v in (g_rate, g_freq, g_re, g_im))
    return (
        output, image_grad, g_rate, g_freq, g_re, g_im, g_step, d_skip, d_gain, d_bias,
        d_win, d_bin, d_wout, d_bout, d_scale,
    )


def solution(mesh):
    tiled = P("th", "tw", None)
    return jax.shard_map(
        per_device,
        mesh=mesh,
        in_specs=(tiled,) + (P(),) * 14 + (tiled,),
        out_specs=(tiled, tiled) + (P(),) * 13,
        check_vma=False,
    )
```

```python
import functools

import jax
import jax.numpy as jnp
import ml_dtypes
import numpy as np
from jax import lax
from jax.experimental import pallas as pl
from jax.experimental.pallas import tpu as pltpu
from jax.sharding import PartitionSpec as P

KSIZE = 15
REACH = KSIZE // 2
EDGE = 8
LANES = 128
GROUP = 16
PAIR = 2
MIB = 2**20
F32, BF16 = jnp.float32, jnp.bfloat16


def swap(block, axis, bit):
    count = lax.axis_size(axis)
    return lax.ppermute(block, axis, [(i, i ^ bit) for i in range(count)])


def swap_across(block, axis):
    count = lax.axis_size(axis)
    pairs = [(i, i + 1) for i in range(1, count - 1, 2)]
    return lax.ppermute(block, axis, pairs + [(j, i) for i, j in pairs])


def tie(value, *others):
    return lax.optimization_barrier((value, *others))[0]


def halo_rows(block):
    place = lax.axis_index("th") % 2
    far = block.shape[0] - REACH
    near = swap(lax.dynamic_slice_in_dim(block, (1 - place) * far, REACH, 0), "th", 1)
    other = swap_across(lax.dynamic_slice_in_dim(block, place * far, REACH, 0), "th")
    return near, other


def halo_cols(*blocks):
    place = lax.axis_index("tw") % 2
    far = blocks[0].shape[1] - EDGE

    def edge(at):
        parts = [lax.dynamic_slice_in_dim(v, at * far, EDGE, 1) for v in blocks]
        return jnp.concatenate(parts, axis=0)

    edges = edge(1 - place), edge(place)
    return swap(edges[0], "tw", 1), swap_across(edges[1], "tw"), edges


def two_parts(matrix):
    high = matrix.astype(ml_dtypes.bfloat16)
    low = (matrix - high.astype(np.float64)).astype(ml_dtypes.bfloat16)
    return np.concatenate([high, low], axis=1)


def transforms(width):
    size = width + 2 * EDGE
    half = size // 2
    place = np.concatenate([EDGE + np.arange(width), np.arange(EDGE), EDGE + width + np.arange(EDGE)])
    freq = np.arange(half)[:, None]

    def angle(n):
        return 2 * np.pi * ((freq * n[None, :]) % size) / size

    lower = -np.sin(angle(place))
    lower[0] = np.cos(np.pi * place)
    forward = np.concatenate([np.cos(angle(place)), lower])
    swapped = np.concatenate([forward[:, :width], forward[:, width + EDGE :], forward[:, width : width + EDGE]], axis=1)

    def back(n):
        real = 2 * np.cos(angle(n)) / size
        imag = -2 * np.sin(angle(n)) / size
        real[0] = 1 / size
        imag[0] = np.cos(np.pi * n) / size
        return np.concatenate([real, imag]).T

    ahead = back(1 + np.arange(width))
    behind = back(KSIZE + np.arange(width))
    lag = np.arange(KSIZE) - REACH
    real, high, imag = (np.zeros((KSIZE + 1, half)) for _ in range(3))
    real[:KSIZE] = (2 * np.cos(angle(lag)) / size).T
    high[:KSIZE] = real[:KSIZE]
    imag[:KSIZE] = (-2 * np.sin(angle(lag)) / size).T
    real[:KSIZE, 0] = 1 / size
    high[:KSIZE, 0] = np.cos(np.pi * lag) / size
    imag[:KSIZE, 0] = 0
    lags = np.concatenate([real, high, imag], axis=1).astype(np.float32)
    tap = np.arange(KSIZE + 1)
    real = np.cos(angle(tap))
    imag = np.sin(angle(tap))
    high = real.copy()
    high[0] = np.cos(np.pi * tap)
    response = np.concatenate([real, imag, high]).astype(np.float32)
    return (
        two_parts(forward), two_parts(swapped), two_parts(forward[:, :width]), two_parts(ahead), two_parts(behind),
        lags, response,
    )


def powers(rate, freq, log_step):
    step = jnp.exp(log_step)
    decay = jnp.exp(-jnp.exp(rate) * step)
    phase = freq * step
    return decay * jnp.cos(phase), decay * jnp.sin(phase), step


def dot(a, b, precision=None, dims=((1,), (0,))):
    return lax.dot_general(a, b, (dims, ((), ())), precision=precision, preferred_element_type=F32)


def taps_kernel(zr_ref, zi_ref, cr_ref, ci_ref, response_ref, taps_ref, factor_ref):
    half = factor_ref.shape[1]
    for d in range(2):
        zr, zi = zr_ref[d], zi_ref[d]
        cr, ci = cr_ref[d], ci_ref[d]
        ur, ui = jnp.ones_like(zr), jnp.zeros_like(zr)
        for m in range(KSIZE):
            taps_ref[d, m] = 2.0 * jnp.sum(cr * ur - ci * ui, axis=0)
            ur, ui = ur * zr - ui * zi, ur * zi + ui * zr
        taps_ref[d, KSIZE] = jnp.zeros_like(taps_ref[d, KSIZE])
    factor = dot(response_ref[...], taps_ref[1], lax.Precision.HIGHEST)
    for k in range(3):
        factor_ref[k] = factor[k * half : (k + 1) * half]


def taps_grad_kernel(
    zr_ref, zi_ref, cr_ref, ci_ref, rate_ref, freq_ref, step_ref, g_ref,
    d_rate_ref, d_freq_ref, d_cr_ref, d_ci_ref, d_step_ref,
):
    for d in range(2):
        zr, zi = zr_ref[d], zi_ref[d]
        cr, ci = cr_ref[d], ci_ref[d]
        ur, ui = jnp.ones_like(zr), jnp.zeros_like(zr)
        su, sv = jnp.zeros_like(zr), jnp.zeros_like(zr)
        mu, mv = jnp.zeros_like(zr), jnp.zeros_like(zr)
        for m in range(KSIZE):
            g = 2.0 * g_ref[d * (KSIZE + 1) + m][None, :]
            gu, gv = g * ur, g * ui
            su, sv = su + gu, sv + gv
            if m:
                mu, mv = mu + float(m) * gu, mv + float(m) * gv
            ur, ui = ur * zr - ui * zi, ur * zi + ui * zr
        step = step_ref[d][None, :]
        freq = freq_ref[d]
        d_freq = -step * (cr * mv + ci * mu)
        d_rate = -jnp.exp(rate_ref[d]) * step * (cr * mu - ci * mv)
        d_cr_ref[d] = su
        d_ci_ref[d] = -sv
        d_freq_ref[d] = d_freq
        d_rate_ref[d] = d_rate
        d_step_ref[d] = jnp.sum(d_rate + freq * d_freq, axis=0)


def load_rows(ext, source_ref, centre, near, other):
    height = centre.shape[0]
    ext[height + 2 * REACH] = jnp.zeros(ext.shape[1:], F32)
    for i in range(REACH):
        ext[source_ref[height * KSIZE] + i] = near[i].astype(F32)
        ext[source_ref[height * KSIZE + 1] + i] = other[i].astype(F32)

    def row(r, _):
        for k in range(4):
            ext[4 * r + k + REACH] = centre[4 * r + k].astype(F32)
        return 0

    lax.fori_loop(0, height // 4, row, 0)


def fold(v):
    return jnp.sum(v.reshape(v.shape[0] // 8, 8, v.shape[1]), axis=0)


def rows_kernel(source_ref, taps_ref, centre, near, other, partial_ref, ext):
    height = centre.shape[0]
    load_rows(ext, source_ref, centre, near, other)
    taps = [taps_ref[0, i][None, :] for i in range(KSIZE)]

    def row(r, _):
        for k in range(2):
            at = 2 * r + k
            total = taps[0] * ext[source_ref[at * KSIZE]]
            for i in range(1, KSIZE):
                total = total + taps[i] * ext[source_ref[at * KSIZE + i]]
            partial_ref[at] = total.astype(BF16)
        return 0

    lax.fori_loop(0, height // 2, row, 0)


def twice(v):
    return jnp.concatenate([v, v], axis=0)


def filtered(spectrum, factor, conjugate):
    half = factor[0].shape[0]
    real, imag = spectrum[:half], spectrum[half:]
    a, b, top = factor
    cross = b * imag
    across = b * real
    if conjugate:
        return jnp.concatenate([a * real + cross, top * imag - across], axis=0).astype(BF16)
    return jnp.concatenate([a * real - cross, top * imag + across], axis=0).astype(BF16)


def side_by_side(values):
    return jnp.concatenate(values, axis=1)


def cols_kernel(
    source_ref, taps_ref, skip_ref, factor_ref, forward_ref, ahead_ref,
    partial_ref, image_ref, near, other,
    mixed_ref, spectrum_ref, sides,
):
    step = pl.program_id(0)
    full = near.shape[0]
    height = full - 2 * REACH
    chans = skip_ref.shape[1]

    @pl.when(step == 0)
    def _():
        sides[full] = jnp.zeros(sides.shape[1:], F32)
        for i in range(2 * REACH):
            base = source_ref[height * KSIZE + i // REACH] + i % REACH
            sides[base] = jnp.concatenate(
                [near[height + i].astype(F32), other[height + i].astype(F32)], axis=0
            )

        def place(r, _):
            for k in range(4):
                at = 4 * r + k
                sides[at + REACH] = jnp.concatenate(
                    [near[at].astype(F32), other[at].astype(F32)], axis=0
                )
            return 0

        lax.fori_loop(0, height // 4, place, 0)

    taps = [taps_ref[0, i][None, :] for i in range(KSIZE)]
    factor = paired(factor_ref)
    skip = skip_ref[...]

    def line(k):
        at = (step * GROUP + k) * KSIZE
        total = taps[0] * sides[source_ref[at]]
        for i in range(1, KSIZE):
            total = total + taps[i] * sides[source_ref[at + i]]
        return jnp.concatenate([partial_ref[k], total.astype(BF16)], axis=0)

    for k in range(0, GROUP, PAIR):
        lines = side_by_side([line(k + n) for n in range(PAIR)])
        spectrum = dot(forward_ref[...], twice(lines))
        mixed = dot(ahead_ref[...], twice(filtered(spectrum, factor, False)))
        for n in range(PAIR):
            cut = slice(n * chans, (n + 1) * chans)
            spectrum_ref[k + n] = spectrum[:, cut].astype(BF16)
            mixed_ref[k + n] = mixed[:, cut] + skip * image_ref[k + n].astype(F32)


def cols_grad_kernel(
    own_ref, lags_ref, d_mixed_ref, spectrum_ref, image_ref, sums_ref, totals, skip_total
):
    step = pl.program_id(0)
    half, chans = totals.shape[1], totals.shape[2]

    @pl.when(step == 0)
    def _():
        totals[...] = jnp.zeros(totals.shape, F32)
        skip_total[...] = jnp.zeros(skip_total.shape, F32)

    for k in range(0, GROUP, PAIR):
        rows = [d_mixed_ref[k + n] for n in range(PAIR)]
        spectra = dot(own_ref[...], twice(side_by_side(rows)))
        found = []
        for n in range(PAIR):
            spectrum = spectra[:, n * chans : (n + 1) * chans]
            real, imag = spectrum[:half], spectrum[half:]
            other = spectrum_ref[k + n].astype(F32)
            other_real, other_imag = other[:half], other[half:]
            found.append((real * other_real, imag * other_imag, real * other_imag - imag * other_real))
            skip_total[...] += fold(rows[n].astype(F32) * image_ref[k + n].astype(F32))
        for m in range(3):
            totals[m] += sum(f[m] for f in found[1:]) + found[0][m]

    @pl.when(step == pl.num_programs(0) - 1)
    def _():
        both = jnp.concatenate([totals[0], totals[1], totals[2]], axis=0)
        sums_ref[...] = dot(lags_ref[...], both, lax.Precision.HIGHEST)
        sums_ref[KSIZE : KSIZE + 1] = jnp.sum(skip_total[...], axis=0, keepdims=True)


def transformed_back(factor, forward_ref, behind_ref, lines):
    chans = factor[0].shape[1] // PAIR
    beside = [jnp.concatenate([near.astype(F32), other.astype(F32)], axis=0).astype(BF16) for _, near, other in lines]
    wide = side_by_side([jnp.concatenate([line[0], side], axis=0) for line, side in zip(lines, beside)])
    spectrum = dot(forward_ref[...], twice(wide))
    some = [f[:, : spectrum.shape[1]] for f in factor]
    found = dot(behind_ref[...], twice(filtered(spectrum, some, True))).astype(BF16)
    return [found[:, n * chans : (n + 1) * chans] for n in range(len(lines))]


def paired(factor_ref):
    return [side_by_side([factor_ref[k]] * PAIR) for k in range(3)]


def cols_back_kernel(
    factor_ref, forward_ref, behind_ref, d_mixed_ref, row_near, col_near, col_other, d_partial_ref, d_near_ref
):
    step = pl.program_id(0)
    height = col_near.shape[0] - REACH
    factor = paired(factor_ref)
    for k in range(0, GROUP, PAIR):
        places = [(k + n, step * GROUP + k + n) for n in range(PAIR)]
        found = transformed_back(
            factor, forward_ref, behind_ref, [(d_mixed_ref[i], col_near[at], col_other[at]) for i, at in places]
        )
        for n in range(PAIR):
            d_partial_ref[k + n] = found[n]

    @pl.when(step == pl.num_programs(0) - 1)
    def _():
        for k in range(0, REACH, PAIR):
            some = range(k, min(k + PAIR, REACH))
            found = transformed_back(
                factor, forward_ref, behind_ref,
                [(row_near[i], col_near[height + i], col_other[height + i]) for i in some],
            )
            for i, value in zip(some, found):
                d_near_ref[i] = value


def strip_back_kernel(factor_ref, forward_ref, behind_ref, rows, near, other, d_rows_ref):
    factor = paired(factor_ref)
    for k in range(0, REACH, PAIR):
        some = range(k, min(k + PAIR, REACH))
        found = transformed_back(
            factor, forward_ref, behind_ref, [(rows[i], near[i], other[i]) for i in some]
        )
        for i, value in zip(some, found):
            d_rows_ref[i] = value


def rows_grad_kernel(source_ref, d_partial_ref, image, near, other, sums_ref, ext):
    height = d_partial_ref.shape[0]
    load_rows(ext, source_ref, image, near, other)

    def row(r, totals):
        totals = list(totals)
        for k in range(2):
            at = 2 * r + k
            d = d_partial_ref[at].astype(F32)
            for i in range(KSIZE):
                totals[i] = totals[i] + fold(d * ext[source_ref[at * KSIZE + i]])
        return tuple(totals)

    zero = jnp.zeros((8, LANES), F32)
    totals = lax.fori_loop(0, height // 2, row, (zero,) * KSIZE)
    for i in range(KSIZE):
        sums_ref[i : i + 1] = jnp.sum(totals[i], axis=0, keepdims=True)
    sums_ref[KSIZE : KSIZE + 1] = jnp.zeros((1, LANES), F32)


def rows_back_kernel(
    first, source_ref, taps_ref, skip_ref, d_partial_ref, near, other, d_mixed_ref, grad_ref, *rest
):
    image_grad_ref, ext = rest[-2:]
    count = d_mixed_ref.shape[0]
    height = d_partial_ref.shape[0]
    ext[height + 2 * REACH] = jnp.zeros(ext.shape[1:], F32)
    for i in range(REACH):
        ext[source_ref[height * KSIZE] + i] = near[i].astype(F32)
        ext[source_ref[height * KSIZE + 1] + i] = other[i].astype(F32)
    low, high = max(first - REACH, 0), min(first + count + REACH, height)

    def place(r, _):
        ext[r + REACH] = d_partial_ref[r].astype(F32)
        return 0

    lax.fori_loop(low, high, place, 0, unroll=3)
    taps = [taps_ref[0, i][None, :] for i in range(KSIZE)]
    skip = skip_ref[...]

    def row(r, _):
        for k in range(2):
            at = 2 * r + k
            total = grad_ref[at].astype(F32) + skip * d_mixed_ref[at].astype(F32)
            for i in range(KSIZE):
                total = total + taps[i] * ext[source_ref[(first + at) * KSIZE + KSIZE - 1 - i]]
            image_grad_ref[at] = total.astype(BF16)
        return 0

    lax.fori_loop(0, count // 2, row, 0)


def feed_kernel(
    mixed_ref, image_ref, grad_ref, w_in_ref, w_out_ref, b_in_ref, gain_ref, bias_ref, b_out_ref, scale_ref,
    output_ref, d_mixed_ref, weights_ref, b_sums_ref, sums_ref,
    act_ref, d_pre_ref,
):
    step = pl.program_id(0)
    chans, hidden = w_in_ref.shape
    piece = 256

    @pl.when(step == 0)
    def _():
        weights_ref[...] = jnp.zeros(weights_ref.shape, F32)
        b_sums_ref[...] = jnp.zeros(b_sums_ref.shape, F32)
        sums_ref[...] = jnp.zeros(sums_ref.shape, F32)

    gain, bias, b_out, scale = (ref[...][None, :] for ref in (gain_ref, bias_ref, b_out_ref, scale_ref))
    b_in = b_in_ref[...][None, :]
    mixed = mixed_ref[...]
    mean = jnp.mean(mixed, axis=-1, keepdims=True)
    centred = mixed - mean
    var = jnp.mean(centred * centred, axis=-1, keepdims=True)
    inverse = lax.rsqrt(var + 1e-06)
    xhat = centred * inverse
    normed = (xhat * gain + bias).astype(BF16)
    grad = grad_ref[...].astype(F32)
    d_branch = (scale * grad).astype(BF16)
    normed_t = jnp.concatenate([normed.T, jnp.ones((16, normed.shape[0]), BF16)], axis=0)
    d_branch_t = d_branch.T
    for k in range(0, hidden, piece):
        cut = slice(k, k + piece)
        pre = dot(normed, w_in_ref[:, cut]) + b_in[:, cut]
        d_act = dot(d_branch, w_out_ref[cut, :], dims=((1,), (1,)))
        half = 0.5 + 0.5 * lax.erf(pre * 0.7071067811865476)
        bell = jnp.exp(pre * pre * -0.5) * 0.3989422804014327
        act = (pre * half).astype(BF16)
        d_pre = (d_act * (half + pre * bell)).astype(BF16)
        act_ref[:, cut] = act
        d_pre_ref[:, cut] = d_pre
        found = dot(normed_t, d_pre)
        weights_ref[0:chans, cut] += found[:chans]
        b_sums_ref[:, cut] += found[chans : chans + 8]
        weights_ref[chans : 2 * chans, cut] += dot(d_branch_t, act)
    branch = dot(w_out_ref[...], act_ref[...], dims=((0,), (1,))).T + b_out
    output_ref[...] = (image_ref[...].astype(F32) + scale * branch).astype(BF16)
    d_normed = dot(w_in_ref[...], d_pre_ref[...], dims=((1,), (1,))).T
    g = d_normed * gain
    g_mean = jnp.mean(g, axis=-1, keepdims=True)
    g_xhat = jnp.mean(g * xhat, axis=-1, keepdims=True)
    d_mixed_ref[...] = ((g - g_mean - xhat * g_xhat) * inverse).astype(BF16)
    sums_ref[0] += fold(d_normed * xhat)
    sums_ref[1] += fold(d_normed)
    sums_ref[2] += fold(d_branch.astype(F32))
    sums_ref[3] += fold(grad * branch)


def whole(shape):
    return pl.BlockSpec(shape, lambda *_: (0,) * len(shape))


def lane_block(*lead):
    return pl.BlockSpec((*lead, LANES), lambda c: (0,) * len(lead) + (c,))


def row_block(*rest):
    return pl.BlockSpec((GROUP, *rest), lambda r: (r,) + (0,) * len(rest))


SCALARS = pl.BlockSpec(memory_space=pltpu.SMEM)


def params():
    return pltpu.CompilerParams(vmem_limit_bytes=60 * MIB)


def cost(us):
    return pl.CostEstimate(flops=int(us * 1e8), bytes_accessed=int(us * 1e5), transcendentals=0)


def mesh_steps():
    def bits(axis):
        return [(axis, 1 << k) for k in range(lax.axis_size(axis).bit_length() - 1)]

    (core, *high), low = bits("th"), bits("tw")
    mixed = [step for pair in zip(high, low) for step in pair]
    return [core] + mixed + high[len(low) :] + low[len(high) :]


def swap_two(block, first, second):
    if first[0] == second[0]:
        return swap(block, first[0], first[1] + second[1])
    bits = dict([first, second])
    high, low = lax.axis_size("th"), lax.axis_size("tw")
    pairs = [
        (i * low + j, (i ^ bits["th"]) * low + (j ^ bits["tw"])) for i in range(high) for j in range(low)
    ]
    return lax.ppermute(block, ("th", "tw"), pairs)


def place_in(steps):
    place = 0
    for n, (axis, bit) in enumerate(steps):
        place = place + lax.rem(lax.axis_index(axis) // bit, 2) * (1 << n)
    return place


def exchanges(steps):
    if len(steps) == 1:
        return [lambda v: swap(v, *steps[0])]
    return [lambda v: swap(v, *steps[0]), lambda v: swap(v, *steps[1]), lambda v: swap_two(v, *steps)]


def scatter(block, steps, kind, beside):
    place = place_in(steps)
    count = 1 << len(steps)
    size = block.shape[0] // count
    total = lax.dynamic_slice_in_dim(block, place * size, size, 0)
    gives = [
        lax.dynamic_slice_in_dim(block, (place ^ k) * size, size, 0).astype(kind) for k in range(1, count)
    ]
    takes = [send(give) for send, give in zip(exchanges(steps), gives)]
    done = beside(gives)
    for take in takes:
        total = total + tie(take, *done).astype(F32)
    return total


def gather(block, steps, beside):
    place = place_in(steps)
    takes = [send(block) for send in exchanges(steps)]
    done = beside([block])
    parts = [block] + [tie(take, *done) for take in takes]
    rows = []
    for q in range(len(parts)):
        found = parts[-1]
        for k in range(len(parts) - 1):
            found = jnp.where((place ^ q) == k, parts[k], found)
        rows.append(found)
    return jnp.concatenate(rows, axis=0)


def finish_kernel(side_ref, own_ref, other_ref, w_in_ref, w_out_ref):
    side = side_ref[0]

    @pl.when(side == 0)
    def _():
        w_in_ref[...] = own_ref[...].astype(F32)
        w_out_ref[...] = other_ref[...].astype(F32).T

    @pl.when(side == 1)
    def _():
        w_in_ref[...] = other_ref[...].astype(F32)
        w_out_ref[...] = own_ref[...].astype(F32).T


def per_device(
    image, image_heights, rate_log, freq, coef_re, coef_im, log_step, skip, ln_gain, ln_bias,
    w_in, b_in, w_out, b_out, layer_scale, out_grad,
):
    height, width, chans = image.shape
    hidden = w_in.shape[1]
    pixels = height * width
    full = height + 2 * REACH
    size = width + 2 * EDGE
    half = size // 2
    blocks = chans // LANES
    groups = height // GROUP
    straight, swapped, own, ahead, behind, lags, response = transforms(width)
    forward = jnp.where(lax.axis_index("tw") % 2 == 1, straight, swapped)

    row_near, row_other = halo_rows(image)
    col_near, col_other, _ = halo_cols(image, row_near, row_other)

    first, second = image_heights[0], image_heights[0] + image_heights[1]
    start = lax.axis_index("th") * height

    def ident(r):
        return (r >= first).astype(jnp.int32) + (r >= second).astype(jnp.int32)

    entry = jnp.arange(height * KSIZE + 2, dtype=jnp.int32)
    row, tap = entry // KSIZE, entry % KSIZE
    source = jnp.where(ident(start + row) == ident(start + row + tap - REACH), row + tap, full)
    place = lax.axis_index("th") % 2
    source = jnp.where(row < height, source, jnp.where(tap == place, REACH + height, 0))

    rate_t, freq_t, cr_t, ci_t = (v.transpose(0, 2, 1) for v in (rate_log, freq, coef_re, coef_im))
    zr, zi, step = powers(rate_t, freq_t, log_step[:, None, :])
    step = step[:, 0]
    taps, factor = pl.pallas_call(
        taps_kernel,
        out_shape=[
            jax.ShapeDtypeStruct((2, KSIZE + 1, chans), F32),
            jax.ShapeDtypeStruct((3, half, chans), F32),
        ],
        name="taps",
    )(zr, zi, cr_t, ci_t, response)

    skip_row = skip[None, :]
    tile_shape = (height, width, chans)
    partial = pl.pallas_call(
        rows_kernel,
        grid=(blocks,),
        in_specs=[
            SCALARS, lane_block(2, KSIZE + 1), lane_block(height, width),
            lane_block(REACH, width), lane_block(REACH, width),
        ],
        out_specs=lane_block(height, width),
        out_shape=jax.ShapeDtypeStruct(tile_shape, BF16),
        scratch_shapes=[pltpu.VMEM((full + 1, width, LANES), F32)],
        compiler_params=params(),
        cost_estimate=cost(14),
        name="rows_forward",
    )(source, taps, image, row_near, row_other)

    mixed, spectrum = pl.pallas_call(
        cols_kernel,
        grid=(groups,),
        in_specs=[
            SCALARS, whole((2, KSIZE + 1, chans)), whole((1, chans)), whole((3, half, chans)),
            whole((size, 2 * size)), whole((width, 2 * size)),
            row_block(width, chans), row_block(width, chans),
            whole((full, EDGE, chans)), whole((full, EDGE, chans)),
        ],
        out_specs=[row_block(width, chans), row_block(size, chans)],
        out_shape=[
            jax.ShapeDtypeStruct(tile_shape, F32),
            jax.ShapeDtypeStruct((height, size, chans), BF16),
        ],
        scratch_shapes=[pltpu.VMEM((full + 1, 2 * EDGE, chans), F32)],
        compiler_params=params(),
        cost_estimate=cost(14),
        name="cols_forward",
    )(
        source, taps, skip_row, factor, forward, ahead, partial, image,
        col_near, col_other,
    )

    tile = 1536
    pixel_block = pl.BlockSpec((tile, chans), lambda i: (i, 0))
    output, d_mixed, weights, b_sums, sums = pl.pallas_call(
        feed_kernel,
        grid=(pixels // tile,),
        in_specs=[
            pixel_block, pixel_block, pixel_block,
            whole((chans, hidden)), whole((hidden, chans)), whole((hidden,)), *[whole((chans,))] * 4,
        ],
        out_specs=[
            pixel_block, pixel_block, whole((2 * chans, hidden)), whole((8, hidden)), whole((4, 8, chans)),
        ],
        out_shape=[
            jax.ShapeDtypeStruct((pixels, chans), BF16),
            jax.ShapeDtypeStruct((pixels, chans), BF16),
            jax.ShapeDtypeStruct((2 * chans, hidden), F32),
            jax.ShapeDtypeStruct((8, hidden), F32),
            jax.ShapeDtypeStruct((4, 8, chans), F32),
        ],
        scratch_shapes=[pltpu.VMEM((tile, hidden), BF16), pltpu.VMEM((tile, hidden), BF16)],
        compiler_params=params(),
        cost_estimate=cost(70),
        name="feed_forward",
    )(
        mixed.reshape(pixels, chans), image.reshape(pixels, chans), out_grad.reshape(pixels, chans),
        w_in, w_out, b_in, ln_gain, ln_bias, b_out, layer_scale,
    )
    output = output.reshape(tile_shape)
    d_mixed = d_mixed.reshape(tile_shape)

    grad_row_near, grad_row_other = halo_rows(d_mixed)
    grad_col_near, grad_col_other, edges = halo_cols(d_mixed, grad_row_near)

    core, *others = mesh_steps()
    phases = [others[k : k + 2] for k in range(0, len(others), 2)]
    found = []

    def cols_grad(sent):
        found.append(
            pl.pallas_call(
                cols_grad_kernel,
                grid=(groups,),
                in_specs=[
                    whole((size, 2 * width)), whole((KSIZE + 1, 3 * half)),
                    row_block(width, chans), row_block(size, chans), row_block(width, chans),
                ],
                out_specs=whole((KSIZE + 1, chans)),
                out_shape=jax.ShapeDtypeStruct((KSIZE + 1, chans), F32),
                scratch_shapes=[pltpu.VMEM((3, half, chans), F32), pltpu.VMEM((8, chans), F32)],
                compiler_params=params(),
                cost_estimate=cost(8),
                name="cols_grad",
            )(own, lags, tie(d_mixed, *sent, *edges), spectrum, image)
        )
        return []

    weights = scatter(weights, [core], F32, cols_grad)
    (col_sums,) = found

    def cols_back(sent):
        found.extend(
            pl.pallas_call(
                cols_back_kernel,
                grid=(groups,),
                in_specs=[
                    whole((3, half, chans)), whole((size, 2 * size)), whole((width, 2 * size)),
                    row_block(width, chans), whole((REACH, width, chans)),
                    whole((full - REACH, EDGE, chans)), whole((full - REACH, EDGE, chans)),
                ],
                out_specs=[row_block(width, chans), whole((REACH, width, chans))],
                out_shape=[
                    jax.ShapeDtypeStruct(tile_shape, BF16),
                    jax.ShapeDtypeStruct((REACH, width, chans), BF16),
                ],
                compiler_params=params(),
                cost_estimate=cost(12),
                name="cols_back",
            )(
                factor, forward, behind, tie(d_mixed, *sent), grad_row_near, grad_col_near, grad_col_other,
            )
        )
        return found[1:]

    weights = scatter(tie(weights, col_sums), phases[0], BF16, cols_back)
    d_partial, d_near = found[1:]
    grad_near_strip, grad_other_strip, strips = halo_cols(tie(grad_row_other, col_sums))

    def rows_grad(sent):
        found.append(
            pl.pallas_call(
                rows_grad_kernel,
                grid=(blocks,),
                in_specs=[
                    SCALARS, lane_block(height, width), lane_block(height, width),
                    lane_block(REACH, width), lane_block(REACH, width),
                ],
                out_specs=lane_block(KSIZE + 1),
                out_shape=jax.ShapeDtypeStruct((KSIZE + 1, chans), F32),
                scratch_shapes=[pltpu.VMEM((full + 1, width, LANES), F32)],
                compiler_params=params(),
                cost_estimate=cost(14),
                name="rows_grad",
            )(source, tie(d_partial, *sent, *strips), image, row_near, row_other)
        )
        return found[-1:]

    weights = scatter(weights, phases[1], F32, rows_grad)
    row_sums = found[-1]
    for later in phases[2:]:
        weights = scatter(weights, later, F32, lambda _: [])
    small = jnp.concatenate(
        [
            tie(row_sums, weights, grad_near_strip, grad_other_strip),
            col_sums, jnp.sum(sums, axis=1), b_sums[0].reshape(hidden // chans, chans),
        ],
        axis=0,
    )
    small = small + swap(small, *core)
    takes = [send(small) for send in exchanges(phases[0])]
    d_other = pl.pallas_call(
        strip_back_kernel,
        out_shape=jax.ShapeDtypeStruct((REACH, width, chans), BF16),
        compiler_params=params(),
        cost_estimate=cost(3),
        name="strip_back",
    )(tie(factor, small), forward, behind, grad_row_other, grad_near_strip, grad_other_strip)
    small = sum([tie(take, d_other) for take in takes], small)

    def rows_back(part, before, *waits):
        count = height // 2
        at = pl.BlockSpec((count, width, LANES), lambda c: (part, 0, c))
        return pl.pallas_call(
            functools.partial(rows_back_kernel, part * count),
            grid=(blocks,),
            in_specs=[
                SCALARS, lane_block(2, KSIZE + 1), lane_block(1), lane_block(height, width),
                lane_block(REACH, width), lane_block(REACH, width), at, at,
                *([] if before is None else [pl.BlockSpec(memory_space=pl.ANY)]),
            ],
            out_specs=at,
            out_shape=jax.ShapeDtypeStruct(tile_shape, BF16),
            scratch_shapes=[pltpu.VMEM((full + 1, width, LANES), F32)],
            compiler_params=params(),
            cost_estimate=cost(8),
            input_output_aliases={} if before is None else {8: 0},
            name="rows_back",
        )(
            source, taps, tie(skip_row, *waits), d_partial, d_near, d_other, d_mixed, out_grad,
            *([] if before is None else [before]),
        )

    weights = weights.astype(BF16)
    backwards = list(reversed(phases))
    early, *late = others[2:]

    def beside(part, *before):
        def work(sent):
            found.append(rows_back(part, *(before or [None]), *sent, small))
            return found[-1:]

        return work

    take = swap(small, *early)
    for n, later in enumerate(backwards[:-1]):
        weights = gather(weights, later, beside(0) if n == 0 else lambda _: [])
    small = small + tie(take, found[-1])
    for later in late[:-1]:
        small = small + swap(small, *later)
    take = swap(small, *late[-1])
    weights = gather(weights, phases[0], beside(1, found[-1]))
    image_grad = found[-1]
    small = small + tie(take, image_grad)
    cut = hidden // 4
    half_block = pl.BlockSpec((chans, cut), lambda k: (0, k))
    d_win, d_wout = pl.pallas_call(
        finish_kernel,
        grid=(4,),
        in_specs=[SCALARS, half_block, half_block],
        out_specs=[half_block, pl.BlockSpec((cut, chans), lambda k: (k, 0))],
        out_shape=[
            jax.ShapeDtypeStruct((chans, hidden), F32),
            jax.ShapeDtypeStruct((hidden, chans), F32),
        ],
        compiler_params=params(),
        cost_estimate=cost(3),
        name="weight_grads",
    )(place_in([core])[None], weights, swap(weights, *core))
    d_skip = small[2 * KSIZE + 1]
    n_sums = 2 * KSIZE + 2
    d_gain, d_bias, d_bout, d_scale = (small[n_sums + i] for i in range(4))
    d_bin = small[n_sums + 4 :].reshape(hidden)

    mode_shape = jax.ShapeDtypeStruct(zr.shape, F32)
    g_rate, g_freq, g_re, g_im, g_step = pl.pallas_call(
        taps_grad_kernel,
        out_shape=[mode_shape] * 4 + [jax.ShapeDtypeStruct((2, chans), F32)],
        name="taps_grad",
    )(zr, zi, cr_t, ci_t, rate_t, freq_t, step, small[:n_sums])
    g_rate, g_freq, g_re, g_im = (v.transpose(0, 2, 1) for v in (g_rate, g_freq, g_re, g_im))
    return (
        output, image_grad, g_rate, g_freq, g_re, g_im, g_step, d_skip, d_gain, d_bias,
        d_win, d_bin, d_wout, d_bout, d_scale,
    )


def solution(mesh):
    tiled = P("th", "tw", None)
    return jax.shard_map(
        per_device,
        mesh=mesh,
        in_specs=(tiled,) + (P(),) * 14 + (tiled,),
        out_specs=(tiled, tiled) + (P(),) * 13,
        check_vma=False,
    )
```

```python
import functools

import jax
import jax.numpy as jnp
import ml_dtypes
import numpy as np
from jax import lax
from jax.experimental import pallas as pl
from jax.experimental.pallas import tpu as pltpu
from jax.sharding import PartitionSpec as P

KSIZE = 15
REACH = KSIZE // 2
EDGE = 8
LANES = 128
GROUP = 16
PAIR = 2
MIB = 2**20
F32, BF16 = jnp.float32, jnp.bfloat16


def swap(block, axis, bit):
    count = lax.axis_size(axis)
    return lax.ppermute(block, axis, [(i, i ^ bit) for i in range(count)])


def swap_across(block, axis):
    count = lax.axis_size(axis)
    pairs = [(i, i + 1) for i in range(1, count - 1, 2)]
    return lax.ppermute(block, axis, pairs + [(j, i) for i, j in pairs])


def tie(value, *others):
    return lax.optimization_barrier((value, *others))[0]


def halo_rows(block):
    place = lax.axis_index("th") % 2
    far = block.shape[0] - REACH
    near = swap(lax.dynamic_slice_in_dim(block, (1 - place) * far, REACH, 0), "th", 1)
    other = swap_across(lax.dynamic_slice_in_dim(block, place * far, REACH, 0), "th")
    return near, other


def halo_cols(*blocks):
    place = lax.axis_index("tw") % 2
    far = blocks[0].shape[1] - EDGE

    def edge(at):
        parts = [lax.dynamic_slice_in_dim(v, at * far, EDGE, 1) for v in blocks]
        return jnp.concatenate(parts, axis=0)

    edges = edge(1 - place), edge(place)
    return swap(edges[0], "tw", 1), swap_across(edges[1], "tw"), edges


def two_parts(matrix):
    high = matrix.astype(ml_dtypes.bfloat16)
    low = (matrix - high.astype(np.float64)).astype(ml_dtypes.bfloat16)
    return np.concatenate([high, low], axis=1)


def transforms(width):
    size = width + 2 * EDGE
    half = size // 2
    place = np.concatenate([EDGE + np.arange(width), np.arange(EDGE), EDGE + width + np.arange(EDGE)])
    freq = np.arange(half)[:, None]

    def angle(n):
        return 2 * np.pi * ((freq * n[None, :]) % size) / size

    lower = -np.sin(angle(place))
    lower[0] = np.cos(np.pi * place)
    forward = np.concatenate([np.cos(angle(place)), lower])
    swapped = np.concatenate([forward[:, :width], forward[:, width + EDGE :], forward[:, width : width + EDGE]], axis=1)

    def back(n):
        real = 2 * np.cos(angle(n)) / size
        imag = -2 * np.sin(angle(n)) / size
        real[0] = 1 / size
        imag[0] = np.cos(np.pi * n) / size
        return np.concatenate([real, imag]).T

    ahead = back(1 + np.arange(width))
    behind = back(KSIZE + np.arange(width))
    lag = np.arange(KSIZE) - REACH
    real, high, imag = (np.zeros((KSIZE + 1, half)) for _ in range(3))
    real[:KSIZE] = (2 * np.cos(angle(lag)) / size).T
    high[:KSIZE] = real[:KSIZE]
    imag[:KSIZE] = (-2 * np.sin(angle(lag)) / size).T
    real[:KSIZE, 0] = 1 / size
    high[:KSIZE, 0] = np.cos(np.pi * lag) / size
    imag[:KSIZE, 0] = 0
    lags = np.concatenate([real, high, imag], axis=1).astype(np.float32)
    tap = np.arange(KSIZE + 1)
    real = np.cos(angle(tap))
    imag = np.sin(angle(tap))
    high = real.copy()
    high[0] = np.cos(np.pi * tap)
    response = np.concatenate([real, imag, high]).astype(np.float32)
    return (
        two_parts(forward), two_parts(swapped), two_parts(forward[:, :width]), two_parts(ahead), two_parts(behind),
        lags, response,
    )


def dot(a, b, precision=None, dims=((1,), (0,))):
    return lax.dot_general(a, b, (dims, ((), ())), precision=precision, preferred_element_type=F32)


def taps_kernel(
    height, heights_ref, rate_ref, freq_ref, cr_ref, ci_ref, log_step_ref, response_ref, straight_ref, swapped_ref,
    taps_ref, factor_ref, forward_ref, source_ref, zr_ref, zi_ref,
):
    half = factor_ref.shape[1]
    for d in range(2):
        step = jnp.exp(log_step_ref[d])[None, :]
        decay = jnp.exp(-jnp.exp(rate_ref[d]) * step)
        phase = freq_ref[d] * step
        zr, zi = decay * jnp.cos(phase), decay * jnp.sin(phase)
        zr_ref[d], zi_ref[d] = zr, zi
        cr, ci = cr_ref[d], ci_ref[d]
        ur, ui = jnp.ones_like(zr), jnp.zeros_like(zr)
        for m in range(KSIZE):
            taps_ref[d, m] = 2.0 * jnp.sum(cr * ur - ci * ui, axis=0)
            ur, ui = ur * zr - ui * zi, ur * zi + ui * zr
        taps_ref[d, KSIZE] = jnp.zeros_like(taps_ref[d, KSIZE])
    factor = dot(response_ref[...], taps_ref[1], lax.Precision.HIGHEST)
    for k in range(3):
        factor_ref[k] = factor[k * half : (k + 1) * half]
    high, right = lax.axis_index("th"), lax.rem(lax.axis_index("tw"), 2)
    place = lax.rem(high, 2)

    @pl.when(right == 1)
    def _():
        forward_ref[...] = straight_ref[...]

    @pl.when(right == 0)
    def _():
        forward_ref[...] = swapped_ref[...]

    row = lax.broadcasted_iota(jnp.int32, source_ref.shape, 0)
    lane = lax.broadcasted_iota(jnp.int32, source_ref.shape, 1)
    first, second = heights_ref[0], heights_ref[0] + heights_ref[1]
    here = row + high * height
    there = here + lane - REACH
    same = ((here >= first) == (there >= first)) & ((here >= second) == (there >= second))
    source = jnp.where(same, row + lane, height + 2 * REACH)
    last = jnp.where(lane == place, REACH + height, 0)
    last = jnp.where(lane == 2, place, jnp.where(lane == 3, right, last))
    source_ref[...] = jnp.where(row < height, source, last)


def taps_grad_kernel(
    zr_ref, zi_ref, cr_ref, ci_ref, rate_ref, freq_ref, step_ref, g_ref,
    d_rate_ref, d_freq_ref, d_cr_ref, d_ci_ref, d_step_ref, d_b_in_ref, *vector_refs,
):
    chans = g_ref.shape[1]
    for k, vector_ref in enumerate(vector_refs):
        vector_ref[...] = g_ref[2 * KSIZE + 1 + k]
    for k in range(d_b_in_ref.shape[0] // chans):
        d_b_in_ref[k * chans : (k + 1) * chans] = g_ref[2 * KSIZE + 1 + len(vector_refs) + k]
    for d in range(2):
        zr, zi = zr_ref[d], zi_ref[d]
        cr, ci = cr_ref[d], ci_ref[d]
        ur, ui = jnp.ones_like(zr), jnp.zeros_like(zr)
        su, sv = jnp.zeros_like(zr), jnp.zeros_like(zr)
        mu, mv = jnp.zeros_like(zr), jnp.zeros_like(zr)
        for m in range(KSIZE):
            g = 2.0 * g_ref[d * (KSIZE + 1) + m][None, :]
            gu, gv = g * ur, g * ui
            su, sv = su + gu, sv + gv
            if m:
                mu, mv = mu + float(m) * gu, mv + float(m) * gv
            ur, ui = ur * zr - ui * zi, ur * zi + ui * zr
        step = jnp.exp(step_ref[d])[None, :]
        freq = freq_ref[d]
        d_freq = -step * (cr * mv + ci * mu)
        d_rate = -jnp.exp(rate_ref[d]) * step * (cr * mu - ci * mv)
        d_cr_ref[d] = su
        d_ci_ref[d] = -sv
        d_freq_ref[d] = d_freq
        d_rate_ref[d] = d_rate
        d_step_ref[d] = jnp.sum(d_rate + freq * d_freq, axis=0)


AHEAD = REACH + 3


def start_rows(ext, source_ref, centre, near, other):
    height = centre.shape[0]
    ext[height + 2 * REACH] = jnp.zeros(ext.shape[1:], F32)
    for i in range(REACH):
        ext[source_ref[height, 0] + i] = near[i].astype(F32)
        ext[source_ref[height, 1] + i] = other[i].astype(F32)
    for i in range(AHEAD):
        ext[REACH + i] = centre[i].astype(F32)


def next_rows(ext, centre, r):
    for k in range(2):
        at = jnp.minimum(2 * r + AHEAD + k, centre.shape[0] - 1)
        ext[REACH + at] = centre[at].astype(F32)


def load_rows(ext, at, centre):
    def place(r, _):
        for k in range(4):
            ext[at + 4 * r + k] = centre[4 * r + k].astype(F32)
        return 0

    lax.fori_loop(0, centre.shape[0] // 4, place, 0)


def fold(v):
    return jnp.sum(v.reshape(v.shape[0] // 8, 8, v.shape[1]), axis=0)


def rows_kernel(source_ref, taps_ref, centre, near, other, partial_ref, ext):
    height = centre.shape[0]
    start_rows(ext, source_ref, centre, near, other)
    load_rows(ext, REACH, centre)
    taps = [taps_ref[0, i][None, :] for i in range(KSIZE)]

    def row(r, _):
        for k in range(4):
            at = 4 * r + k
            total = taps[0] * ext[source_ref[at, 0]]
            for i in range(1, KSIZE):
                total = total + taps[i] * ext[source_ref[at, i]]
            partial_ref[at] = total.astype(BF16)
        return 0

    lax.fori_loop(0, height // 4, row, 0)


def twice(v):
    return jnp.concatenate([v, v], axis=0)


def filtered(spectrum, factor, conjugate):
    half = factor[0].shape[0]
    real, imag = spectrum[:half], spectrum[half:]
    a, b, top = factor
    cross = b * imag
    across = b * real
    if conjugate:
        return jnp.concatenate([a * real + cross, top * imag - across], axis=0).astype(BF16)
    return jnp.concatenate([a * real - cross, top * imag + across], axis=0).astype(BF16)


def side_by_side(values):
    return jnp.concatenate(values, axis=1)


def cols_kernel(
    source_ref, taps_ref, skip_ref, factor_ref, forward_ref, ahead_ref,
    partial_ref, image_ref, near, other, near_strip, other_strip,
    mixed_ref, spectrum_ref, sides,
):
    step = pl.program_id(0)
    height = near.shape[0]
    full = height + 2 * REACH
    chans = skip_ref.shape[0]

    @pl.when(step == 0)
    def _():
        sides[full] = jnp.zeros(sides.shape[1:], F32)
        for i in range(2 * REACH):
            base = source_ref[height, i // REACH] + i % REACH
            sides[base] = jnp.concatenate(
                [near_strip[i].astype(F32), other_strip[i].astype(F32)], axis=0
            )

        def place(r, _):
            for k in range(4):
                at = 4 * r + k
                sides[at + REACH] = jnp.concatenate(
                    [near[at].astype(F32), other[at].astype(F32)], axis=0
                )
            return 0

        lax.fori_loop(0, height // 4, place, 0)

    taps = [taps_ref[0, i][None, :] for i in range(KSIZE)]
    factor = paired(factor_ref)
    skip = skip_ref[...][None, :]

    def line(k):
        at = step * GROUP + k
        total = taps[0] * sides[source_ref[at, 0]]
        for i in range(1, KSIZE):
            total = total + taps[i] * sides[source_ref[at, i]]
        return jnp.concatenate([partial_ref[k], total.astype(BF16)], axis=0)

    for k in range(0, GROUP, PAIR):
        lines = side_by_side([line(k + n) for n in range(PAIR)])
        spectrum = dot(forward_ref[...], twice(lines))
        mixed = dot(ahead_ref[...], twice(filtered(spectrum, factor, False)))
        for n in range(PAIR):
            cut = slice(n * chans, (n + 1) * chans)
            spectrum_ref[k + n] = spectrum[:, cut].astype(BF16)
            mixed_ref[k + n] = mixed[:, cut] + skip * image_ref[k + n].astype(F32)


def cols_grad_kernel(
    own_ref, lags_ref, d_mixed_ref, spectrum_ref, image_ref, sums_ref, totals, skip_total
):
    step = pl.program_id(0)
    half, chans = totals.shape[1], totals.shape[2]

    @pl.when(step == 0)
    def _():
        totals[...] = jnp.zeros(totals.shape, F32)
        skip_total[...] = jnp.zeros(skip_total.shape, F32)

    for k in range(0, GROUP, PAIR):
        rows = [d_mixed_ref[k + n] for n in range(PAIR)]
        spectra = dot(own_ref[...], twice(side_by_side(rows)))
        found = []
        for n in range(PAIR):
            spectrum = spectra[:, n * chans : (n + 1) * chans]
            real, imag = spectrum[:half], spectrum[half:]
            other = spectrum_ref[k + n].astype(F32)
            other_real, other_imag = other[:half], other[half:]
            found.append((real * other_real, imag * other_imag, real * other_imag - imag * other_real))
            skip_total[...] += fold(rows[n].astype(F32) * image_ref[k + n].astype(F32))
        for m in range(3):
            totals[m] += sum(f[m] for f in found[1:]) + found[0][m]

    @pl.when(step == pl.num_programs(0) - 1)
    def _():
        both = jnp.concatenate([totals[0], totals[1], totals[2]], axis=0)
        sums_ref[...] = dot(lags_ref[...], both, lax.Precision.HIGHEST)
        sums_ref[KSIZE : KSIZE + 1] = jnp.sum(skip_total[...], axis=0, keepdims=True)


def transformed_back(factor, forward_ref, behind_ref, lines):
    chans = factor[0].shape[1] // PAIR
    beside = [jnp.concatenate([near.astype(F32), other.astype(F32)], axis=0).astype(BF16) for _, near, other in lines]
    wide = side_by_side([jnp.concatenate([line[0], side], axis=0) for line, side in zip(lines, beside)])
    spectrum = dot(forward_ref[...], twice(wide))
    some = [f[:, : spectrum.shape[1]] for f in factor]
    found = dot(behind_ref[...], twice(filtered(spectrum, some, True))).astype(BF16)
    return [found[:, n * chans : (n + 1) * chans] for n in range(len(lines))]


def paired(factor_ref):
    return [side_by_side([factor_ref[k]] * PAIR) for k in range(3)]


def cols_back_kernel(
    source_ref, factor_ref, forward_ref, behind_ref, d_mixed_ref, near, other, d_partial_ref, near_give, other_give
):
    step = pl.program_id(0)
    last = pl.num_programs(0) - 1
    factor = paired(factor_ref)
    for k in range(0, GROUP, PAIR):
        places = range(k, k + PAIR)
        found = transformed_back(
            factor, forward_ref, behind_ref, [(d_mixed_ref[i], near[i], other[i]) for i in places]
        )
        for i, value in zip(places, found):
            d_partial_ref[i] = value
    high = source_ref[GROUP * pl.num_programs(0), 2]
    for at, where, side in ((0, 0, 1), (last, GROUP - REACH, 0)):
        for to, place in ((near_give, side), (other_give, 1 - side)):

            @pl.when((step == at) & (high == place))
            def _():
                to[...] = d_partial_ref[where : where + REACH]


def rows_grad_kernel(source_ref, d_partial_ref, image, near, other, sums_ref, ext):
    height = d_partial_ref.shape[0]
    start_rows(ext, source_ref, image, near, other)

    def row(r, totals):
        totals = list(totals)
        for k in range(2):
            at = 2 * r + k
            d = d_partial_ref[at].astype(F32)
            for i in range(KSIZE):
                totals[i] = totals[i] + fold(d * ext[source_ref[at, i]])
        next_rows(ext, image, r)
        return tuple(totals)

    zero = jnp.zeros((8, LANES), F32)
    totals = lax.fori_loop(0, height // 2, row, (zero,) * KSIZE)
    for i in range(KSIZE):
        sums_ref[i : i + 1] = jnp.sum(totals[i], axis=0, keepdims=True)
    sums_ref[KSIZE : KSIZE + 1] = jnp.zeros((1, LANES), F32)


def rows_back_kernel(
    first, source_ref, taps_ref, skip_ref, d_partial_ref, beside, near, other, d_mixed_ref, grad_ref, *rest
):
    image_grad_ref, ext = rest[-2:]
    count = d_partial_ref.shape[0]
    height = 2 * count
    ext[height + 2 * REACH] = jnp.zeros(ext.shape[1:], F32)
    for i in range(REACH):
        ext[source_ref[height, 0] + i] = near[i].astype(F32)
        ext[source_ref[height, 1] + i] = other[i].astype(F32)
    beyond = count if first == 0 else count - EDGE
    for i in range(EDGE):
        ext[REACH + beyond + i] = beside[i].astype(F32)
    load_rows(ext, REACH + first, d_partial_ref)
    taps = [taps_ref[0, i][None, :] for i in range(KSIZE)]
    skip = skip_ref[...]

    def row(r, _):
        for k in range(4):
            at = 4 * r + k
            total = grad_ref[at].astype(F32) + skip * d_mixed_ref[at].astype(F32)
            for i in range(KSIZE):
                total = total + taps[i] * ext[source_ref[first + at, KSIZE - 1 - i]]
            image_grad_ref[at] = total.astype(BF16)
        return 0

    lax.fori_loop(0, count // 4, row, 0)


def feed_kernel(
    source_ref, mixed_ref, image_ref, grad_ref, w_in_ref, w_out_ref, b_in_ref, gain_ref, bias_ref, b_out_ref, scale_ref,
    output_ref, d_mixed_ref, col_near_ref, col_other_ref, keep_ref, give_ref,
    pieces_ref, b_sums_ref, sums_ref, act_ref, d_pre_ref, weights_ref,
):
    step = pl.program_id(0)
    last = pl.num_programs(0) - 1
    chans, hidden = w_in_ref.shape
    piece = 256
    pixels = d_mixed_ref.shape[0]
    lines = col_near_ref.shape[0] // EDGE
    width = pixels // lines
    height = lines * pl.num_programs(0)
    high, right = source_ref[height, 2], source_ref[height, 3]

    @pl.when(step == 0)
    def _():
        weights_ref[...] = jnp.zeros(weights_ref.shape, F32)
        b_sums_ref[...] = jnp.zeros(b_sums_ref.shape, F32)
        sums_ref[...] = jnp.zeros(sums_ref.shape, F32)

    gain, bias, b_out, scale = (ref[...][None, :] for ref in (gain_ref, bias_ref, b_out_ref, scale_ref))
    b_in = b_in_ref[...][None, :]
    mixed = mixed_ref[...]
    mean = jnp.mean(mixed, axis=-1, keepdims=True)
    centred = mixed - mean
    var = jnp.mean(centred * centred, axis=-1, keepdims=True)
    inverse = lax.rsqrt(var + 1e-06)
    xhat = centred * inverse
    normed = (xhat * gain + bias).astype(BF16)
    grad = grad_ref[...].astype(F32)
    d_branch = (scale * grad).astype(BF16)
    normed_t = jnp.concatenate([normed.T, jnp.ones((16, normed.shape[0]), BF16)], axis=0)
    d_branch_t = d_branch.T

    def inward(k):
        cut = slice(k, k + piece)
        pre = dot(normed, w_in_ref[:, cut]) + b_in[:, cut]
        return pre, dot(d_branch, w_out_ref[cut, :], dims=((1,), (1,)))

    ahead = inward(0)
    for k in range(0, hidden, piece):
        cut = slice(k, k + piece)
        pre, d_act = ahead
        if k + piece < hidden:
            ahead = inward(k + piece)
        half = 0.5 + 0.5 * lax.erf(pre * 0.7071067811865476)
        bell = jnp.exp(pre * pre * -0.5) * 0.3989422804014327
        act = (pre * half).astype(BF16)
        d_pre = (d_act * (half + pre * bell)).astype(BF16)
        act_ref[:, cut] = act
        d_pre_ref[:, cut] = d_pre
        found = dot(normed_t, d_pre)
        weights_ref[0:chans, cut] += found[:chans]
        b_sums_ref[:, cut] += found[chans : chans + 8]
        weights_ref[chans : 2 * chans, cut] += dot(d_branch_t, act)
    branch = dot(w_out_ref[...], act_ref[...], dims=((0,), (1,))).T + b_out
    output_ref[...] = (image_ref[...].astype(F32) + scale * branch).astype(BF16)
    d_normed = dot(w_in_ref[...], d_pre_ref[...], dims=((1,), (1,))).T
    g = d_normed * gain
    g_mean = jnp.mean(g, axis=-1, keepdims=True)
    g_xhat = jnp.mean(g * xhat, axis=-1, keepdims=True)
    d_mixed = (g - g_mean - xhat * g_xhat) * inverse
    d_mixed_ref[...] = d_mixed.astype(BF16)
    grid = d_mixed.reshape(lines, width, chans)
    left = grid[:, :EDGE].reshape(col_near_ref.shape)
    far = grid[:, width - EDGE :].reshape(col_near_ref.shape)
    col_near_ref[...] = jnp.where(right == 1, left, far).astype(BF16)
    col_other_ref[...] = jnp.where(right == 1, far, left).astype(BF16)
    sums_ref[0] += fold(d_normed * xhat)
    sums_ref[1] += fold(d_normed)
    sums_ref[2] += fold(d_branch.astype(F32))
    sums_ref[3] += fold(grad * branch)

    @pl.when(step == last)
    def _():
        for place in range(2):

            @pl.when(high == place)
            def _():
                keep_ref[...] = weights_ref[place * chans : (place + 1) * chans]
                give_ref[...] = weights_ref[(1 - place) * chans : (2 - place) * chans].astype(BF16)

        pieces_ref[0:4] = jnp.sum(sums_ref[...], axis=1)
        for k in range(hidden // chans):
            pieces_ref[4 + k : 5 + k] = b_sums_ref[0:1, k * chans : (k + 1) * chans]


def whole(shape):
    return pl.BlockSpec(shape, lambda *_: (0,) * len(shape))


def lane_block(*lead):
    return pl.BlockSpec((*lead, LANES), lambda c: (0,) * len(lead) + (c,))


def row_block(*rest):
    return pl.BlockSpec((GROUP, *rest), lambda r: (r,) + (0,) * len(rest))


SCALARS = pl.BlockSpec(memory_space=pltpu.SMEM)


def params(mib=60):
    return pltpu.CompilerParams(vmem_limit_bytes=mib * MIB)


def cost(us):
    return pl.CostEstimate(flops=int(us * 1e6), bytes_accessed=int(us * 1e3), transcendentals=0)


def mesh_steps():
    def bits(axis):
        return [(axis, 1 << k) for k in range(lax.axis_size(axis).bit_length() - 1)]

    (core, *high), low = bits("th"), bits("tw")
    mixed = [step for pair in zip(high, low) for step in pair]
    return [core] + mixed + high[len(low) :] + low[len(high) :]


def swap_two(block, first, second):
    if first[0] == second[0]:
        return swap(block, first[0], first[1] + second[1])
    bits = dict([first, second])
    high, low = lax.axis_size("th"), lax.axis_size("tw")
    pairs = [
        (i * low + j, (i ^ bits["th"]) * low + (j ^ bits["tw"])) for i in range(high) for j in range(low)
    ]
    return lax.ppermute(block, ("th", "tw"), pairs)


def place_in(steps):
    place = 0
    for n, (axis, bit) in enumerate(steps):
        place = place + lax.rem(lax.axis_index(axis) // bit, 2) * (1 << n)
    return place


def exchanges(steps):
    if len(steps) == 1:
        return [lambda v: swap(v, *steps[0])]
    return [lambda v: swap(v, *steps[0]), lambda v: swap(v, *steps[1]), lambda v: swap_two(v, *steps)]


def scatter(block, steps, beside):
    place = place_in(steps)
    size = block.shape[0] >> len(steps)
    parts = [lax.dynamic_slice_in_dim(block, (place ^ k) * size, size, 0) for k in range(1 << len(steps))]
    takes = [send(part) for send, part in zip(exchanges(steps), parts[1:])]
    done = beside(parts[1:])
    return sum([tie(take, *done) for take in takes], parts[0])


def gather(block, steps, beside):
    place = place_in(steps)
    takes = [send(block) for send in exchanges(steps)]
    done = beside([block])
    parts = [block] + [tie(take, *done) for take in takes]
    rows = []
    for q in range(len(parts)):
        found = parts[-1]
        for k in range(len(parts) - 1):
            found = jnp.where((place ^ q) == k, parts[k], found)
        rows.append(found)
    return jnp.concatenate(rows, axis=0)


def split_kernel(place_ref, keep_ref, take_ref, own_ref, *give_refs):
    size = own_ref.shape[0]
    for k, to in enumerate((own_ref, *give_refs)):
        rows = pl.ds(pl.multiple_of((place_ref[0] ^ k) * size, size), size)
        to[...] = (keep_ref[rows] + take_ref[rows].astype(F32)).astype(to.dtype)


def finish_kernel(side_ref, own_ref, other_ref, w_in_ref, w_out_ref):
    side = side_ref[0]

    @pl.when(side == 0)
    def _():
        w_in_ref[...] = own_ref[...].astype(F32)
        w_out_ref[...] = other_ref[...].T.astype(F32)

    @pl.when(side == 1)
    def _():
        w_in_ref[...] = other_ref[...].astype(F32)
        w_out_ref[...] = own_ref[...].T.astype(F32)


def per_device(
    image, image_heights, rate_log, freq, coef_re, coef_im, log_step, skip, ln_gain, ln_bias,
    w_in, b_in, w_out, b_out, layer_scale, out_grad,
):
    height, width, chans = image.shape
    hidden = w_in.shape[1]
    pixels = height * width
    full = height + 2 * REACH
    size = width + 2 * EDGE
    half = size // 2
    blocks = chans // LANES
    groups = height // GROUP
    straight, swapped, own, ahead, behind, lags, response = transforms(width)

    row_near, row_other = halo_rows(image)
    col_near, col_other, edges = halo_cols(image)

    rate_t, freq_t, cr_t, ci_t = (v.transpose(0, 2, 1) for v in (rate_log, freq, coef_re, coef_im))
    mode_shape = jax.ShapeDtypeStruct(rate_t.shape, F32)
    vmem = pl.BlockSpec(memory_space=pltpu.VMEM)
    taps, factor, forward, source, zr, zi = pl.pallas_call(
        functools.partial(taps_kernel, height),
        in_specs=[SCALARS] + [vmem] * 8,
        out_shape=[
            jax.ShapeDtypeStruct((2, KSIZE + 1, chans), F32),
            jax.ShapeDtypeStruct((3, half, chans), F32),
            jax.ShapeDtypeStruct((size, 2 * size), BF16),
            jax.ShapeDtypeStruct((height + 8, LANES), jnp.int32),
            mode_shape,
            mode_shape,
        ],
        cost_estimate=cost(5),
        name="taps",
    )(image_heights, rate_t, freq_t, cr_t, ci_t, tie(log_step, *edges), response, straight, swapped)

    near_strip, other_strip, strips = halo_cols(row_near, tie(row_other, taps))
    tile_shape = (height, width, chans)
    partial = pl.pallas_call(
        rows_kernel,
        grid=(blocks,),
        in_specs=[
            SCALARS, lane_block(2, KSIZE + 1), lane_block(height, width),
            lane_block(REACH, width), lane_block(REACH, width),
        ],
        out_specs=lane_block(height, width),
        out_shape=jax.ShapeDtypeStruct(tile_shape, BF16),
        scratch_shapes=[pltpu.VMEM((full + 1, width, LANES), F32)],
        compiler_params=params(),
        cost_estimate=cost(14),
        name="rows_forward",
    )(source, tie(taps, *strips), image, row_near, row_other)

    mixed, spectrum = pl.pallas_call(
        cols_kernel,
        grid=(groups,),
        in_specs=[
            SCALARS, whole((2, KSIZE + 1, chans)), whole((chans,)), whole((3, half, chans)),
            whole((size, 2 * size)), whole((width, 2 * size)),
            row_block(width, chans), row_block(width, chans),
            whole((height, EDGE, chans)), whole((height, EDGE, chans)),
            whole((2 * REACH, EDGE, chans)), whole((2 * REACH, EDGE, chans)),
        ],
        out_specs=[row_block(width, chans), row_block(size, chans)],
        out_shape=[
            jax.ShapeDtypeStruct(tile_shape, F32),
            jax.ShapeDtypeStruct((height, size, chans), BF16),
        ],
        scratch_shapes=[pltpu.VMEM((full + 1, 2 * EDGE, chans), F32)],
        compiler_params=params(),
        cost_estimate=cost(14),
        name="cols_forward",
    )(
        source, taps, skip, factor, forward, ahead, partial, image,
        col_near, col_other, near_strip, other_strip,
    )

    tile = 1536
    pixel_block = pl.BlockSpec((tile, chans), lambda i: (i, 0))
    col_block = pl.BlockSpec((tile // width * EDGE, chans), lambda i: (i, 0))
    output, d_mixed, col_near_give, col_other_give, keep, give, pieces = pl.pallas_call(
        feed_kernel,
        grid=(pixels // tile,),
        in_specs=[
            SCALARS, pixel_block, pixel_block, pixel_block,
            whole((chans, hidden)), whole((hidden, chans)), whole((hidden,)), *[whole((chans,))] * 4,
        ],
        out_specs=[
            pixel_block, pixel_block, col_block, col_block,
            whole((chans, hidden)), whole((chans, hidden)), whole((4 + hidden // chans, chans)),
        ],
        out_shape=[
            jax.ShapeDtypeStruct((pixels, chans), BF16),
            jax.ShapeDtypeStruct((pixels, chans), BF16),
            jax.ShapeDtypeStruct((height * EDGE, chans), BF16),
            jax.ShapeDtypeStruct((height * EDGE, chans), BF16),
            jax.ShapeDtypeStruct((chans, hidden), F32),
            jax.ShapeDtypeStruct((chans, hidden), BF16),
            jax.ShapeDtypeStruct((4 + hidden // chans, chans), F32),
        ],
        scratch_shapes=[
            pltpu.VMEM((8, hidden), F32), pltpu.VMEM((4, 8, chans), F32),
            pltpu.VMEM((tile, hidden), BF16), pltpu.VMEM((tile, hidden), BF16), pltpu.VMEM((2 * chans, hidden), F32),
        ],
        compiler_params=params(),
        cost_estimate=cost(70),
        name="feed_forward",
    )(
        source, mixed.reshape(pixels, chans), image.reshape(pixels, chans), out_grad.reshape(pixels, chans),
        w_in, w_out, b_in, ln_gain, ln_bias, b_out, layer_scale,
    )
    output = output.reshape(tile_shape)
    d_mixed = d_mixed.reshape(tile_shape)

    col_shape = (height, EDGE, chans)
    grad_col_near = swap(col_near_give, "tw", 1).reshape(col_shape)
    grad_col_other = swap_across(col_other_give, "tw").reshape(col_shape)

    core, *others = mesh_steps()
    phases = [others[k : k + 2] for k in range(0, len(others), 2)]
    take = swap(give, *core)
    col_sums = pl.pallas_call(
        cols_grad_kernel,
        grid=(groups,),
        in_specs=[
            whole((size, 2 * width)), whole((KSIZE + 1, 3 * half)),
            row_block(width, chans), row_block(size, chans), row_block(width, chans),
        ],
        out_specs=whole((KSIZE + 1, chans)),
        out_shape=jax.ShapeDtypeStruct((KSIZE + 1, chans), F32),
        scratch_shapes=[pltpu.VMEM((3, half, chans), F32), pltpu.VMEM((8, chans), F32)],
        compiler_params=params(),
        cost_estimate=cost(8),
        name="cols_grad",
    )(own, lags, d_mixed, spectrum, image)
    found = [col_sums]
    parts = 1 << len(phases[0])
    own_part, *gives = pl.pallas_call(
        split_kernel,
        in_specs=[SCALARS, vmem, vmem],
        out_shape=[
            jax.ShapeDtypeStruct((chans // parts, hidden), F32 if k == 0 else BF16) for k in range(parts)
        ],
        compiler_params=params(16),
        cost_estimate=cost(2),
        name="split",
    )(place_in(phases[0])[None], keep, tie(take, col_sums))

    edge = (REACH, width, chans)

    def cols_back(sent):
        found.extend(
            pl.pallas_call(
                cols_back_kernel,
                grid=(groups,),
                in_specs=[
                    SCALARS, whole((3, half, chans)), whole((size, 2 * size)), whole((width, 2 * size)),
                    row_block(width, chans), row_block(EDGE, chans), row_block(EDGE, chans),
                ],
                out_specs=[row_block(width, chans), whole(edge), whole(edge)],
                out_shape=[
                    jax.ShapeDtypeStruct(tile_shape, BF16),
                    jax.ShapeDtypeStruct(edge, BF16),
                    jax.ShapeDtypeStruct(edge, BF16),
                ],
                compiler_params=params(),
                cost_estimate=cost(12),
                name="cols_back",
            )(source, factor, forward, behind, tie(d_mixed, *sent), grad_col_near, grad_col_other)
        )
        return found[1:]

    takes = [send(part) for send, part in zip(exchanges(phases[0]), gives)]
    done = cols_back(gives)
    weights = sum([tie(part, *done).astype(F32) for part in takes], own_part)
    d_partial, near_give, other_give = found[1:]
    d_near = swap(near_give, "th", 1)
    d_other = swap_across(other_give, "th")

    def rows_grad(sent):
        found.append(
            pl.pallas_call(
                rows_grad_kernel,
                grid=(blocks,),
                in_specs=[
                    SCALARS, lane_block(height, width), lane_block(height, width),
                    lane_block(REACH, width), lane_block(REACH, width),
                ],
                out_specs=lane_block(KSIZE + 1),
                out_shape=jax.ShapeDtypeStruct((KSIZE + 1, chans), F32),
                scratch_shapes=[pltpu.VMEM((full + 1, width, LANES), F32)],
                compiler_params=params(),
                cost_estimate=cost(14),
                name="rows_grad",
            )(source, tie(d_partial, *sent), image, row_near, row_other)
        )
        return found[-1:]

    for n, later in enumerate(phases[1:]):
        weights = scatter(weights, later, rows_grad if n == 0 else lambda _: [])
    row_sums = found[-1]
    small = jnp.concatenate([tie(row_sums, weights, d_near, d_other), col_sums, pieces], axis=0)
    small = small + swap(small, *core)
    weights = weights.astype(BF16)
    for later in reversed(phases[1:]):
        weights = gather(weights, later, lambda _: [small])
    takes = [send(small) for send in exchanges(phases[0])]
    small = sum(takes, small)

    skip_row = tie(skip, give)[None, :]

    def rows_back(part, before, *waits):
        count = height // 2
        lanes = lambda rows, block=0: pl.BlockSpec((rows, width, LANES), lambda c: (block, 0, c))
        at = lanes(count, part)
        return pl.pallas_call(
            functools.partial(rows_back_kernel, part * count),
            grid=(blocks,),
            in_specs=[
                SCALARS, lane_block(2, KSIZE + 1), lane_block(1), at, lanes(EDGE, count // EDGE - part),
                lanes(REACH), lanes(REACH), at, at,
                *([] if before is None else [pl.BlockSpec(memory_space=pl.ANY)]),
            ],
            out_specs=at,
            out_shape=jax.ShapeDtypeStruct(tile_shape, BF16),
            scratch_shapes=[pltpu.VMEM((full + 1, width, LANES), F32)],
            compiler_params=params(),
            cost_estimate=cost(8),
            input_output_aliases={} if before is None else {9: 0},
            name="rows_back",
        )(
            source, taps, tie(skip_row, *waits), d_partial, d_partial, d_near, d_other, d_mixed, out_grad,
            *([] if before is None else [before]),
        )

    for n, later in enumerate(phases[1:]):
        takes = [send(small) for send in exchanges(later)]
        if n == 0:
            image_grad = rows_back(0, None, small)
        small = sum([tie(take, image_grad) for take in takes], small)

    def last_rows(sent):
        found.append(rows_back(1, image_grad, *sent))
        return found[-1:]

    weights = gather(tie(weights, small), phases[0], last_rows)
    image_grad = found[-1]
    cut = hidden // 4
    half_block = pl.BlockSpec((chans, cut), lambda k: (0, k))
    d_win, d_wout = pl.pallas_call(
        finish_kernel,
        grid=(4,),
        in_specs=[SCALARS, half_block, half_block],
        out_specs=[half_block, pl.BlockSpec((cut, chans), lambda k: (k, 0))],
        out_shape=[
            jax.ShapeDtypeStruct((chans, hidden), F32),
            jax.ShapeDtypeStruct((hidden, chans), F32),
        ],
        compiler_params=params(16),
        cost_estimate=cost(3),
        name="weight_grads",
    )(place_in([core])[None], weights, swap(weights, *core))
    vector = jax.ShapeDtypeStruct((chans,), F32)
    g_rate, g_freq, g_re, g_im, g_step, d_bin, d_skip, d_gain, d_bias, d_bout, d_scale = pl.pallas_call(
        taps_grad_kernel,
        out_shape=[mode_shape] * 4
        + [jax.ShapeDtypeStruct((2, chans), F32), jax.ShapeDtypeStruct((hidden,), F32)]
        + [vector] * 5,
        cost_estimate=cost(3),
        name="taps_grad",
    )(zr, zi, cr_t, ci_t, rate_t, freq_t, log_step, small)
    g_rate, g_freq, g_re, g_im = (v.transpose(0, 2, 1) for v in (g_rate, g_freq, g_re, g_im))
    return (
        output, image_grad, g_rate, g_freq, g_re, g_im, g_step, d_skip, d_gain, d_bias,
        d_win, d_bin, d_wout, d_bout, d_scale,
    )


def solution(mesh):
    tiled = P("th", "tw", None)
    return jax.shard_map(
        per_device,
        mesh=mesh,
        in_specs=(tiled,) + (P(),) * 14 + (tiled,),
        out_specs=(tiled, tiled) + (P(),) * 13,
        check_vma=False,
    )
```

```python
import functools

import jax
import jax.numpy as jnp
import ml_dtypes
import numpy as np
from jax import lax
from jax.experimental import pallas as pl
from jax.experimental.pallas import tpu as pltpu
from jax.sharding import PartitionSpec as P

KSIZE = 15
REACH = KSIZE // 2
EDGE = 8
LANES = 128
GROUP = 16
PAIR = 2
MIB = 2**20
F32, BF16 = jnp.float32, jnp.bfloat16


def swap(block, axis, bit):
    count = lax.axis_size(axis)
    return lax.ppermute(block, axis, [(i, i ^ bit) for i in range(count)])


def swap_across(block, axis):
    count = lax.axis_size(axis)
    pairs = [(i, i + 1) for i in range(1, count - 1, 2)]
    return lax.ppermute(block, axis, pairs + [(j, i) for i, j in pairs])


def tie(value, *others):
    return lax.optimization_barrier((value, *others))[0]


def halo_rows(block):
    place = lax.axis_index("th") % 2
    far = block.shape[0] - REACH
    near = swap(lax.dynamic_slice_in_dim(block, (1 - place) * far, REACH, 0), "th", 1)
    other = swap_across(lax.dynamic_slice_in_dim(block, place * far, REACH, 0), "th")
    return near, other


def halo_cols(*blocks):
    place = lax.axis_index("tw") % 2
    far = blocks[0].shape[1] - EDGE

    def edge(at):
        parts = [lax.dynamic_slice_in_dim(v, at * far, EDGE, 1) for v in blocks]
        return jnp.concatenate(parts, axis=0)

    edges = edge(1 - place), edge(place)
    return swap(edges[0], "tw", 1), swap_across(edges[1], "tw"), edges


def two_parts(matrix):
    high = matrix.astype(ml_dtypes.bfloat16)
    low = (matrix - high.astype(np.float64)).astype(ml_dtypes.bfloat16)
    return np.concatenate([high, low], axis=1)


def transforms(width):
    size = width + 2 * EDGE
    half = size // 2
    place = np.concatenate([EDGE + np.arange(width), np.arange(EDGE), EDGE + width + np.arange(EDGE)])
    freq = np.arange(half)[:, None]

    def angle(n):
        return 2 * np.pi * ((freq * n[None, :]) % size) / size

    lower = -np.sin(angle(place))
    lower[0] = np.cos(np.pi * place)
    forward = np.concatenate([np.cos(angle(place)), lower])
    swapped = np.concatenate([forward[:, :width], forward[:, width + EDGE :], forward[:, width : width + EDGE]], axis=1)

    def back(n):
        real = 2 * np.cos(angle(n)) / size
        imag = -2 * np.sin(angle(n)) / size
        real[0] = 1 / size
        imag[0] = np.cos(np.pi * n) / size
        return np.concatenate([real, imag]).T

    ahead = back(1 + np.arange(width))
    behind = back(KSIZE + np.arange(width))
    lag = np.arange(KSIZE) - REACH
    real, high, imag = (np.zeros((KSIZE + 1, half)) for _ in range(3))
    real[:KSIZE] = (2 * np.cos(angle(lag)) / size).T
    high[:KSIZE] = real[:KSIZE]
    imag[:KSIZE] = (-2 * np.sin(angle(lag)) / size).T
    real[:KSIZE, 0] = 1 / size
    high[:KSIZE, 0] = np.cos(np.pi * lag) / size
    imag[:KSIZE, 0] = 0
    lags = np.concatenate([real, high, imag], axis=1).astype(np.float32)
    tap = np.arange(KSIZE + 1)
    real = np.cos(angle(tap))
    imag = np.sin(angle(tap))
    high = real.copy()
    high[0] = np.cos(np.pi * tap)
    response = np.concatenate([real, imag, high]).astype(np.float32)
    return (
        two_parts(forward), two_parts(swapped), two_parts(forward[:, :width]), two_parts(ahead), two_parts(behind),
        lags, response,
    )


def dot(a, b, precision=None, dims=((1,), (0,))):
    return lax.dot_general(a, b, (dims, ((), ())), precision=precision, preferred_element_type=F32)


def taps_kernel(
    height, heights_ref, rate_ref, freq_ref, cr_ref, ci_ref, log_step_ref, skip_ref, response_ref, straight_ref, swapped_ref,
    taps_ref, factor_ref, forward_ref, source_ref, zr_ref, zi_ref,
):
    half = factor_ref.shape[1]
    for d in range(2):
        step = jnp.exp(log_step_ref[d])[None, :]
        decay = jnp.exp(-jnp.exp(rate_ref[d]) * step)
        phase = freq_ref[d] * step
        zr, zi = decay * jnp.cos(phase), decay * jnp.sin(phase)
        zr_ref[d], zi_ref[d] = zr, zi
        cr, ci = cr_ref[d], ci_ref[d]
        ur, ui = jnp.ones_like(zr), jnp.zeros_like(zr)
        for m in range(KSIZE):
            taps_ref[d, m] = 2.0 * jnp.sum(cr * ur - ci * ui, axis=0)
            ur, ui = ur * zr - ui * zi, ur * zi + ui * zr
    taps_ref[0, KSIZE] = skip_ref[...]
    taps_ref[1, KSIZE] = jnp.zeros_like(skip_ref[...])
    factor = dot(response_ref[...], taps_ref[1], lax.Precision.HIGHEST)
    for k in range(3):
        factor_ref[k] = factor[k * half : (k + 1) * half]
    high, right = lax.axis_index("th"), lax.rem(lax.axis_index("tw"), 2)
    place = lax.rem(high, 2)

    @pl.when(right == 1)
    def _():
        forward_ref[...] = straight_ref[...]

    @pl.when(right == 0)
    def _():
        forward_ref[...] = swapped_ref[...]

    row = lax.broadcasted_iota(jnp.int32, source_ref.shape, 0)
    lane = lax.broadcasted_iota(jnp.int32, source_ref.shape, 1)
    first, second = heights_ref[0], heights_ref[0] + heights_ref[1]
    here = row + high * height
    there = here + lane - REACH
    same = ((here >= first) == (there >= first)) & ((here >= second) == (there >= second))
    source = jnp.where(same, row + lane, height + 2 * REACH)
    last = jnp.where(lane == place, REACH + height, 0)
    last = jnp.where(lane == 2, place, jnp.where(lane == 3, right, last))
    source_ref[...] = jnp.where(row < height, source, last)


def taps_grad_kernel(
    zr_ref, zi_ref, cr_ref, ci_ref, rate_ref, freq_ref, step_ref, g_ref,
    d_rate_ref, d_freq_ref, d_cr_ref, d_ci_ref, d_step_ref, d_b_in_ref, *vector_refs,
):
    chans = g_ref.shape[1]
    for k, vector_ref in enumerate(vector_refs):
        vector_ref[...] = g_ref[2 * KSIZE + 1 + k]
    for k in range(d_b_in_ref.shape[0] // chans):
        d_b_in_ref[k * chans : (k + 1) * chans] = g_ref[2 * KSIZE + 1 + len(vector_refs) + k]
    for d in range(2):
        zr, zi = zr_ref[d], zi_ref[d]
        cr, ci = cr_ref[d], ci_ref[d]
        ur, ui = jnp.ones_like(zr), jnp.zeros_like(zr)
        su, sv = jnp.zeros_like(zr), jnp.zeros_like(zr)
        mu, mv = jnp.zeros_like(zr), jnp.zeros_like(zr)
        for m in range(KSIZE):
            g = 2.0 * g_ref[d * (KSIZE + 1) + m][None, :]
            gu, gv = g * ur, g * ui
            su, sv = su + gu, sv + gv
            if m:
                mu, mv = mu + float(m) * gu, mv + float(m) * gv
            ur, ui = ur * zr - ui * zi, ur * zi + ui * zr
        step = jnp.exp(step_ref[d])[None, :]
        freq = freq_ref[d]
        d_freq = -step * (cr * mv + ci * mu)
        d_rate = -jnp.exp(rate_ref[d]) * step * (cr * mu - ci * mv)
        d_cr_ref[d] = su
        d_ci_ref[d] = -sv
        d_freq_ref[d] = d_freq
        d_rate_ref[d] = d_rate
        d_step_ref[d] = jnp.sum(d_rate + freq * d_freq, axis=0)


AHEAD = REACH + 3


def start_rows(ext, source_ref, centre, near, other):
    height = centre.shape[0]
    ext[height + 2 * REACH] = jnp.zeros(ext.shape[1:], F32)
    for i in range(REACH):
        ext[source_ref[height, 0] + i] = near[i].astype(F32)
        ext[source_ref[height, 1] + i] = other[i].astype(F32)
    for i in range(AHEAD):
        ext[REACH + i] = centre[i].astype(F32)


def next_rows(ext, centre, r):
    for k in range(2):
        at = jnp.minimum(2 * r + AHEAD + k, centre.shape[0] - 1)
        ext[REACH + at] = centre[at].astype(F32)


def load_rows(ext, at, centre):
    def place(r, _):
        for k in range(4):
            ext[at + 4 * r + k] = centre[4 * r + k].astype(F32)
        return 0

    lax.fori_loop(0, centre.shape[0] // 4, place, 0)


def fold(v):
    return jnp.sum(v.reshape(v.shape[0] // 8, 8, v.shape[1]), axis=0)


def rows_kernel(source_ref, taps_ref, centre, near, other, partial_ref, ext):
    height = centre.shape[0]
    start_rows(ext, source_ref, centre, near, other)
    load_rows(ext, REACH, centre)
    taps = [taps_ref[0, i][None, :] for i in range(KSIZE)]

    def row(r, _):
        for k in range(4):
            at = 4 * r + k
            total = taps[0] * ext[source_ref[at, 0]]
            for i in range(1, KSIZE):
                total = total + taps[i] * ext[source_ref[at, i]]
            partial_ref[at] = total.astype(BF16)
        return 0

    lax.fori_loop(0, height // 4, row, 0)


def twice(v):
    return jnp.concatenate([v, v], axis=0)


def filtered(spectrum, factor, conjugate):
    half = factor[0].shape[0]
    real, imag = spectrum[:half], spectrum[half:]
    a, b, top = factor
    cross = b * imag
    across = b * real
    if conjugate:
        return jnp.concatenate([a * real + cross, top * imag - across], axis=0).astype(BF16)
    return jnp.concatenate([a * real - cross, top * imag + across], axis=0).astype(BF16)


def side_by_side(values):
    return jnp.concatenate(values, axis=1)


def cols_kernel(
    source_ref, taps_ref, skip_ref, factor_ref, forward_ref, ahead_ref,
    partial_ref, image_ref, near, other, near_strip, other_strip,
    mixed_ref, spectrum_ref, sides,
):
    step = pl.program_id(0)
    height = near.shape[0]
    full = height + 2 * REACH
    chans = skip_ref.shape[0]

    @pl.when(step == 0)
    def _():
        sides[full] = jnp.zeros(sides.shape[1:], F32)
        for i in range(2 * REACH):
            base = source_ref[height, i // REACH] + i % REACH
            sides[base] = jnp.concatenate(
                [near_strip[i].astype(F32), other_strip[i].astype(F32)], axis=0
            )

        def place(r, _):
            for k in range(4):
                at = 4 * r + k
                sides[at + REACH] = jnp.concatenate(
                    [near[at].astype(F32), other[at].astype(F32)], axis=0
                )
            return 0

        lax.fori_loop(0, height // 4, place, 0)

    taps = [taps_ref[0, i][None, :] for i in range(KSIZE)]
    factor = paired(factor_ref)
    skip = skip_ref[...][None, :]

    def line(k):
        at = step * GROUP + k
        total = taps[0] * sides[source_ref[at, 0]]
        for i in range(1, KSIZE):
            total = total + taps[i] * sides[source_ref[at, i]]
        return jnp.concatenate([partial_ref[k], total.astype(BF16)], axis=0)

    for k in range(0, GROUP, PAIR):
        lines = side_by_side([line(k + n) for n in range(PAIR)])
        spectrum = dot(forward_ref[...], twice(lines))
        mixed = dot(ahead_ref[...], twice(filtered(spectrum, factor, False)))
        for n in range(PAIR):
            cut = slice(n * chans, (n + 1) * chans)
            spectrum_ref[k + n] = spectrum[:, cut].astype(BF16)
            mixed_ref[k + n] = mixed[:, cut] + skip * image_ref[k + n].astype(F32)


def cols_grad_kernel(
    own_ref, lags_ref, d_mixed_ref, spectrum_ref, image_ref, sums_ref, totals, skip_total
):
    step = pl.program_id(0)
    half, chans = totals.shape[1], totals.shape[2]

    @pl.when(step == 0)
    def _():
        totals[...] = jnp.zeros(totals.shape, F32)
        skip_total[...] = jnp.zeros(skip_total.shape, F32)

    for k in range(0, GROUP, PAIR):
        rows = [d_mixed_ref[k + n] for n in range(PAIR)]
        spectra = dot(own_ref[...], twice(side_by_side(rows)))
        found = []
        for n in range(PAIR):
            spectrum = spectra[:, n * chans : (n + 1) * chans]
            real, imag = spectrum[:half], spectrum[half:]
            other = spectrum_ref[k + n].astype(F32)
            other_real, other_imag = other[:half], other[half:]
            found.append((real * other_real, imag * other_imag, real * other_imag - imag * other_real))
            skip_total[...] += fold(rows[n].astype(F32) * image_ref[k + n].astype(F32))
        for m in range(3):
            totals[m] += sum(f[m] for f in found[1:]) + found[0][m]

    @pl.when(step == pl.num_programs(0) - 1)
    def _():
        both = jnp.concatenate([totals[0], totals[1], totals[2]], axis=0)
        sums_ref[...] = dot(lags_ref[...], both, lax.Precision.HIGHEST)
        sums_ref[KSIZE : KSIZE + 1] = jnp.sum(skip_total[...], axis=0, keepdims=True)


def transformed_back(factor, forward_ref, behind_ref, lines):
    chans = factor[0].shape[1] // PAIR
    beside = [jnp.concatenate([near.astype(F32), other.astype(F32)], axis=0).astype(BF16) for _, near, other in lines]
    wide = side_by_side([jnp.concatenate([line[0], side], axis=0) for line, side in zip(lines, beside)])
    spectrum = dot(forward_ref[...], twice(wide))
    some = [f[:, : spectrum.shape[1]] for f in factor]
    found = dot(behind_ref[...], twice(filtered(spectrum, some, True))).astype(BF16)
    return [found[:, n * chans : (n + 1) * chans] for n in range(len(lines))]


def paired(factor_ref):
    return [side_by_side([factor_ref[k]] * PAIR) for k in range(3)]


def cols_back_kernel(
    source_ref, factor_ref, forward_ref, behind_ref, d_mixed_ref, near, other, d_partial_ref, near_give, other_give
):
    step = pl.program_id(0)
    last = pl.num_programs(0) - 1
    factor = paired(factor_ref)
    for k in range(0, GROUP, PAIR):
        places = range(k, k + PAIR)
        found = transformed_back(
            factor, forward_ref, behind_ref, [(d_mixed_ref[i], near[i], other[i]) for i in places]
        )
        for i, value in zip(places, found):
            d_partial_ref[i] = value
    high = source_ref[GROUP * pl.num_programs(0), 2]
    for at, where, side in ((0, 0, 1), (last, GROUP - REACH, 0)):
        for to, place in ((near_give, side), (other_give, 1 - side)):

            @pl.when((step == at) & (high == place))
            def _():
                to[...] = d_partial_ref[where : where + REACH]


def rows_grad_kernel(source_ref, d_partial_ref, image, near, other, sums_ref, ext):
    height = d_partial_ref.shape[0]
    start_rows(ext, source_ref, image, near, other)

    def row(r, totals):
        totals = list(totals)
        for k in range(2):
            at = 2 * r + k
            d = d_partial_ref[at].astype(F32)
            for i in range(KSIZE):
                totals[i] = totals[i] + fold(d * ext[source_ref[at, i]])
        next_rows(ext, image, r)
        return tuple(totals)

    zero = jnp.zeros((8, LANES), F32)
    totals = lax.fori_loop(0, height // 2, row, (zero,) * KSIZE)
    for i in range(KSIZE):
        sums_ref[i : i + 1] = jnp.sum(totals[i], axis=0, keepdims=True)
    sums_ref[KSIZE : KSIZE + 1] = jnp.zeros((1, LANES), F32)


def rows_back_kernel(
    first, source_ref, taps_ref, d_partial_ref, beside, near, other, d_mixed_ref, grad_ref, *rest
):
    image_grad_ref, ext = rest[-2:]
    count = d_partial_ref.shape[0]
    height = 2 * count
    ext[height + 2 * REACH] = jnp.zeros(ext.shape[1:], F32)
    for i in range(REACH):
        ext[source_ref[height, 0] + i] = near[i].astype(F32)
        ext[source_ref[height, 1] + i] = other[i].astype(F32)
    beyond = count if first == 0 else count - EDGE
    for i in range(EDGE):
        ext[REACH + beyond + i] = beside[i].astype(F32)
    load_rows(ext, REACH + first, d_partial_ref)
    taps = [taps_ref[0, i][None, :] for i in range(KSIZE)]
    skip = taps_ref[0, KSIZE][None, :]

    def row(r, _):
        for k in range(4):
            at = 4 * r + k
            total = grad_ref[at].astype(F32) + skip * d_mixed_ref[at].astype(F32)
            for i in range(KSIZE):
                total = total + taps[i] * ext[source_ref[first + at, KSIZE - 1 - i]]
            image_grad_ref[at] = total.astype(BF16)
        return 0

    lax.fori_loop(0, count // 4, row, 0)


def feed_kernel(
    source_ref, mixed_ref, image_ref, grad_ref, w_in_ref, w_out_ref, b_in_ref, gain_ref, bias_ref, b_out_ref, scale_ref,
    output_ref, d_mixed_ref, col_near_ref, col_other_ref, keep_ref, give_ref,
    pieces_ref, b_sums_ref, sums_ref, act_ref, d_pre_ref, weights_ref,
):
    step = pl.program_id(0)
    last = pl.num_programs(0) - 1
    chans, hidden = w_in_ref.shape
    piece = 256
    pixels = d_mixed_ref.shape[0]
    lines = col_near_ref.shape[0] // EDGE
    width = pixels // lines
    height = lines * pl.num_programs(0)
    high, right = source_ref[height, 2], source_ref[height, 3]

    @pl.when(step == 0)
    def _():
        weights_ref[...] = jnp.zeros(weights_ref.shape, F32)
        b_sums_ref[...] = jnp.zeros(b_sums_ref.shape, F32)
        sums_ref[...] = jnp.zeros(sums_ref.shape, F32)

    gain, bias, b_out, scale = (ref[...][None, :] for ref in (gain_ref, bias_ref, b_out_ref, scale_ref))
    b_in = b_in_ref[...][None, :]
    mixed = mixed_ref[...]
    mean = jnp.mean(mixed, axis=-1, keepdims=True)
    centred = mixed - mean
    var = jnp.mean(centred * centred, axis=-1, keepdims=True)
    inverse = lax.rsqrt(var + 1e-06)
    xhat = centred * inverse
    normed = (xhat * gain + bias).astype(BF16)
    grad = grad_ref[...].astype(F32)
    d_branch = (scale * grad).astype(BF16)
    normed_t = jnp.concatenate([normed.T, jnp.ones((16, normed.shape[0]), BF16)], axis=0)
    d_branch_t = d_branch.T

    def inward(k):
        cut = slice(k, k + piece)
        pre = dot(normed, w_in_ref[:, cut]) + b_in[:, cut]
        return pre, dot(d_branch, w_out_ref[cut, :], dims=((1,), (1,)))

    ahead = inward(0)
    for k in range(0, hidden, piece):
        cut = slice(k, k + piece)
        pre, d_act = ahead
        if k + piece < hidden:
            ahead = inward(k + piece)
        half = 0.5 + 0.5 * lax.erf(pre * 0.7071067811865476)
        bell = jnp.exp(pre * pre * -0.5) * 0.3989422804014327
        act = (pre * half).astype(BF16)
        d_pre = (d_act * (half + pre * bell)).astype(BF16)
        act_ref[:, cut] = act
        d_pre_ref[:, cut] = d_pre
        found = dot(normed_t, d_pre)
        weights_ref[0:chans, cut] += found[:chans]
        b_sums_ref[:, cut] += found[chans : chans + 8]
        weights_ref[chans : 2 * chans, cut] += dot(d_branch_t, act)
    branch = dot(w_out_ref[...], act_ref[...], dims=((0,), (1,))).T + b_out
    output_ref[...] = (image_ref[...].astype(F32) + scale * branch).astype(BF16)
    d_normed = dot(w_in_ref[...], d_pre_ref[...], dims=((1,), (1,))).T
    g = d_normed * gain
    g_mean = jnp.mean(g, axis=-1, keepdims=True)
    g_xhat = jnp.mean(g * xhat, axis=-1, keepdims=True)
    d_mixed = (g - g_mean - xhat * g_xhat) * inverse
    d_mixed_ref[...] = d_mixed.astype(BF16)
    grid = d_mixed.reshape(lines, width, chans)
    left = grid[:, :EDGE].reshape(col_near_ref.shape)
    far = grid[:, width - EDGE :].reshape(col_near_ref.shape)
    col_near_ref[...] = jnp.where(right == 1, left, far).astype(BF16)
    col_other_ref[...] = jnp.where(right == 1, far, left).astype(BF16)
    sums_ref[0] += fold(d_normed * xhat)
    sums_ref[1] += fold(d_normed)
    sums_ref[2] += fold(d_branch.astype(F32))
    sums_ref[3] += fold(grad * branch)

    @pl.when(step == last)
    def _():
        for place in range(2):

            @pl.when(high == place)
            def _():
                keep_ref[...] = weights_ref[place * chans : (place + 1) * chans]
                give_ref[...] = weights_ref[(1 - place) * chans : (2 - place) * chans].astype(BF16)

        pieces_ref[0:4] = jnp.sum(sums_ref[...], axis=1)
        for k in range(hidden // chans):
            pieces_ref[4 + k : 5 + k] = b_sums_ref[0:1, k * chans : (k + 1) * chans]


def whole(shape):
    return pl.BlockSpec(shape, lambda *_: (0,) * len(shape))


def lane_block(*lead):
    return pl.BlockSpec((*lead, LANES), lambda c: (0,) * len(lead) + (c,))


def row_block(*rest):
    return pl.BlockSpec((GROUP, *rest), lambda r: (r,) + (0,) * len(rest))


SCALARS = pl.BlockSpec(memory_space=pltpu.SMEM)


def params(mib=60):
    return pltpu.CompilerParams(vmem_limit_bytes=mib * MIB)


def cost(us):
    return pl.CostEstimate(flops=int(us * 1e6), bytes_accessed=int(us * 1e3), transcendentals=0)


def mesh_steps():
    def bits(axis):
        return [(axis, 1 << k) for k in range(lax.axis_size(axis).bit_length() - 1)]

    (core, *high), low = bits("th"), bits("tw")
    mixed = [step for pair in zip(high, low) for step in pair]
    return [core] + mixed + high[len(low) :] + low[len(high) :]


def swap_two(block, first, second):
    if first[0] == second[0]:
        return swap(block, first[0], first[1] + second[1])
    bits = dict([first, second])
    high, low = lax.axis_size("th"), lax.axis_size("tw")
    pairs = [
        (i * low + j, (i ^ bits["th"]) * low + (j ^ bits["tw"])) for i in range(high) for j in range(low)
    ]
    return lax.ppermute(block, ("th", "tw"), pairs)


def place_in(steps):
    place = 0
    for n, (axis, bit) in enumerate(steps):
        place = place + lax.rem(lax.axis_index(axis) // bit, 2) * (1 << n)
    return place


def exchanges(steps):
    if len(steps) == 1:
        return [lambda v: swap(v, *steps[0])]
    return [lambda v: swap(v, *steps[0]), lambda v: swap(v, *steps[1]), lambda v: swap_two(v, *steps)]


def scatter(block, steps, beside):
    place = place_in(steps)
    size = block.shape[0] >> len(steps)
    parts = [lax.dynamic_slice_in_dim(block, (place ^ k) * size, size, 0) for k in range(1 << len(steps))]
    takes = [send(part) for send, part in zip(exchanges(steps), parts[1:])]
    done = beside(parts[1:])
    return sum([tie(take, *done) for take in takes], parts[0])


def gather(block, steps, beside):
    place = place_in(steps)
    takes = [send(block) for send in exchanges(steps)]
    done = beside([block])
    parts = [block] + [tie(take, *done) for take in takes]
    rows = []
    for q in range(len(parts)):
        found = parts[-1]
        for k in range(len(parts) - 1):
            found = jnp.where((place ^ q) == k, parts[k], found)
        rows.append(found)
    return jnp.concatenate(rows, axis=0)


def split_kernel(place_ref, keep_ref, take_ref, own_ref, *give_refs):
    size = own_ref.shape[0]
    for k, to in enumerate((own_ref, *give_refs)):
        rows = pl.ds(pl.multiple_of((place_ref[0] ^ k) * size, size), size)
        to[...] = (keep_ref[rows] + take_ref[rows].astype(F32)).astype(to.dtype)


def finish_kernel(side_ref, own_ref, other_ref, w_in_ref, w_out_ref):
    side = side_ref[0]

    @pl.when(side == 0)
    def _():
        w_in_ref[...] = own_ref[...].astype(F32)
        w_out_ref[...] = other_ref[...].T.astype(F32)

    @pl.when(side == 1)
    def _():
        w_in_ref[...] = other_ref[...].astype(F32)
        w_out_ref[...] = own_ref[...].T.astype(F32)


def per_device(
    image, image_heights, rate_log, freq, coef_re, coef_im, log_step, skip, ln_gain, ln_bias,
    w_in, b_in, w_out, b_out, layer_scale, out_grad,
):
    height, width, chans = image.shape
    hidden = w_in.shape[1]
    pixels = height * width
    full = height + 2 * REACH
    size = width + 2 * EDGE
    half = size // 2
    blocks = chans // LANES
    groups = height // GROUP
    straight, swapped, own, ahead, behind, lags, response = transforms(width)

    row_near, row_other = halo_rows(image)
    col_near, col_other, edges = halo_cols(image)

    rate_t, freq_t, cr_t, ci_t = (v.transpose(0, 2, 1) for v in (rate_log, freq, coef_re, coef_im))
    mode_shape = jax.ShapeDtypeStruct(rate_t.shape, F32)
    vmem = pl.BlockSpec(memory_space=pltpu.VMEM)
    taps, factor, forward, source, zr, zi = pl.pallas_call(
        functools.partial(taps_kernel, height),
        in_specs=[SCALARS] + [vmem] * 9,
        out_shape=[
            jax.ShapeDtypeStruct((2, KSIZE + 1, chans), F32),
            jax.ShapeDtypeStruct((3, half, chans), F32),
            jax.ShapeDtypeStruct((size, 2 * size), BF16),
            jax.ShapeDtypeStruct((height + 8, LANES), jnp.int32),
            mode_shape,
            mode_shape,
        ],
        cost_estimate=cost(5),
        name="taps",
    )(image_heights, rate_t, freq_t, cr_t, ci_t, tie(log_step, *edges), skip, response, straight, swapped)

    near_strip, other_strip, strips = halo_cols(row_near, tie(row_other, taps))
    tile_shape = (height, width, chans)
    partial = pl.pallas_call(
        rows_kernel,
        grid=(blocks,),
        in_specs=[
            SCALARS, lane_block(2, KSIZE + 1), lane_block(height, width),
            lane_block(REACH, width), lane_block(REACH, width),
        ],
        out_specs=lane_block(height, width),
        out_shape=jax.ShapeDtypeStruct(tile_shape, BF16),
        scratch_shapes=[pltpu.VMEM((full + 1, width, LANES), F32)],
        compiler_params=params(),
        cost_estimate=cost(14),
        name="rows_forward",
    )(source, tie(taps, *strips), image, row_near, row_other)

    mixed, spectrum = pl.pallas_call(
        cols_kernel,
        grid=(groups,),
        in_specs=[
            SCALARS, whole((2, KSIZE + 1, chans)), whole((chans,)), whole((3, half, chans)),
            whole((size, 2 * size)), whole((width, 2 * size)),
            row_block(width, chans), row_block(width, chans),
            whole((height, EDGE, chans)), whole((height, EDGE, chans)),
            whole((2 * REACH, EDGE, chans)), whole((2 * REACH, EDGE, chans)),
        ],
        out_specs=[row_block(width, chans), row_block(size, chans)],
        out_shape=[
            jax.ShapeDtypeStruct(tile_shape, F32),
            jax.ShapeDtypeStruct((height, size, chans), BF16),
        ],
        scratch_shapes=[pltpu.VMEM((full + 1, 2 * EDGE, chans), F32)],
        compiler_params=params(),
        cost_estimate=cost(14),
        name="cols_forward",
    )(
        source, taps, skip, factor, forward, ahead, partial, image,
        col_near, col_other, near_strip, other_strip,
    )

    tile = 1536
    pixel_block = pl.BlockSpec((tile, chans), lambda i: (i, 0))
    col_block = pl.BlockSpec((tile // width * EDGE, chans), lambda i: (i, 0))
    output, d_mixed, col_near_give, col_other_give, keep, give, pieces = pl.pallas_call(
        feed_kernel,
        grid=(pixels // tile,),
        in_specs=[
            SCALARS, pixel_block, pixel_block, pixel_block,
            whole((chans, hidden)), whole((hidden, chans)), whole((hidden,)), *[whole((chans,))] * 4,
        ],
        out_specs=[
            pixel_block, pixel_block, col_block, col_block,
            whole((chans, hidden)), whole((chans, hidden)), whole((4 + hidden // chans, chans)),
        ],
        out_shape=[
            jax.ShapeDtypeStruct((pixels, chans), BF16),
            jax.ShapeDtypeStruct((pixels, chans), BF16),
            jax.ShapeDtypeStruct((height * EDGE, chans), BF16),
            jax.ShapeDtypeStruct((height * EDGE, chans), BF16),
            jax.ShapeDtypeStruct((chans, hidden), F32),
            jax.ShapeDtypeStruct((chans, hidden), BF16),
            jax.ShapeDtypeStruct((4 + hidden // chans, chans), F32),
        ],
        scratch_shapes=[
            pltpu.VMEM((8, hidden), F32), pltpu.VMEM((4, 8, chans), F32),
            pltpu.VMEM((tile, hidden), BF16), pltpu.VMEM((tile, hidden), BF16), pltpu.VMEM((2 * chans, hidden), F32),
        ],
        compiler_params=params(),
        cost_estimate=cost(70),
        name="feed_forward",
    )(
        source, mixed.reshape(pixels, chans), image.reshape(pixels, chans), out_grad.reshape(pixels, chans),
        w_in, w_out, b_in, ln_gain, ln_bias, b_out, layer_scale,
    )
    output = output.reshape(tile_shape)
    d_mixed = d_mixed.reshape(tile_shape)

    col_shape = (height, EDGE, chans)
    grad_col_near = swap(col_near_give, "tw", 1).reshape(col_shape)
    grad_col_other = swap_across(col_other_give, "tw").reshape(col_shape)

    core, *others = mesh_steps()
    phases = [others[k : k + 2] for k in range(0, len(others), 2)]
    take = swap(give, *core)
    col_sums = pl.pallas_call(
        cols_grad_kernel,
        grid=(groups,),
        in_specs=[
            whole((size, 2 * width)), whole((KSIZE + 1, 3 * half)),
            row_block(width, chans), row_block(size, chans), row_block(width, chans),
        ],
        out_specs=whole((KSIZE + 1, chans)),
        out_shape=jax.ShapeDtypeStruct((KSIZE + 1, chans), F32),
        scratch_shapes=[pltpu.VMEM((3, half, chans), F32), pltpu.VMEM((8, chans), F32)],
        compiler_params=params(),
        cost_estimate=cost(8),
        name="cols_grad",
    )(own, lags, d_mixed, spectrum, image)
    found = [col_sums]
    parts = 1 << len(phases[0])
    own_part, *gives = pl.pallas_call(
        split_kernel,
        in_specs=[SCALARS, vmem, vmem],
        out_shape=[
            jax.ShapeDtypeStruct((chans // parts, hidden), F32 if k == 0 else BF16) for k in range(parts)
        ],
        compiler_params=params(16),
        cost_estimate=cost(2),
        name="split",
    )(place_in(phases[0])[None], keep, tie(take, col_sums))

    edge = (REACH, width, chans)

    def cols_back(sent):
        found.extend(
            pl.pallas_call(
                cols_back_kernel,
                grid=(groups,),
                in_specs=[
                    SCALARS, whole((3, half, chans)), whole((size, 2 * size)), whole((width, 2 * size)),
                    row_block(width, chans), row_block(EDGE, chans), row_block(EDGE, chans),
                ],
                out_specs=[row_block(width, chans), whole(edge), whole(edge)],
                out_shape=[
                    jax.ShapeDtypeStruct(tile_shape, BF16),
                    jax.ShapeDtypeStruct(edge, BF16),
                    jax.ShapeDtypeStruct(edge, BF16),
                ],
                compiler_params=params(),
                cost_estimate=cost(12),
                name="cols_back",
            )(source, factor, forward, behind, tie(d_mixed, *sent), grad_col_near, grad_col_other)
        )
        return found[1:]

    takes = [send(part) for send, part in zip(exchanges(phases[0]), gives)]
    done = cols_back(gives)
    weights = sum([tie(part, *done).astype(F32) for part in takes], own_part)
    d_partial, near_give, other_give = found[1:]
    d_near = swap(near_give, "th", 1)
    d_other = swap_across(other_give, "th")

    def rows_grad(sent):
        found.append(
            pl.pallas_call(
                rows_grad_kernel,
                grid=(blocks,),
                in_specs=[
                    SCALARS, lane_block(height, width), lane_block(height, width),
                    lane_block(REACH, width), lane_block(REACH, width),
                ],
                out_specs=lane_block(KSIZE + 1),
                out_shape=jax.ShapeDtypeStruct((KSIZE + 1, chans), F32),
                scratch_shapes=[pltpu.VMEM((full + 1, width, LANES), F32)],
                compiler_params=params(),
                cost_estimate=cost(14),
                name="rows_grad",
            )(source, tie(d_partial, *sent), image, row_near, row_other)
        )
        return found[-1:]

    for n, later in enumerate(phases[1:]):
        weights = scatter(weights, later, rows_grad if n == 0 else lambda _: [])
    row_sums = found[-1]
    small = jnp.concatenate([tie(row_sums, weights, d_near, d_other), col_sums, pieces], axis=0)
    small = small + swap(small, *core)
    weights = weights.astype(BF16)
    for later in reversed(phases[1:]):
        weights = gather(weights, later, lambda _: [small])
    takes = [send(small) for send in exchanges(phases[0])]
    small = sum(takes, small)

    def rows_back(part, before, *waits):
        count = height // 2
        lanes = lambda rows, block=0: pl.BlockSpec((rows, width, LANES), lambda c: (block, 0, c))
        at = lanes(count, part)
        return pl.pallas_call(
            functools.partial(rows_back_kernel, part * count),
            grid=(blocks,),
            in_specs=[
                SCALARS, lane_block(2, KSIZE + 1), at, lanes(EDGE, count // EDGE - part),
                lanes(REACH), lanes(REACH), at, at,
                *([] if before is None else [pl.BlockSpec(memory_space=pl.ANY)]),
            ],
            out_specs=at,
            out_shape=jax.ShapeDtypeStruct(tile_shape, BF16),
            scratch_shapes=[pltpu.VMEM((full + 1, width, LANES), F32)],
            compiler_params=params(),
            cost_estimate=cost(8),
            input_output_aliases={} if before is None else {8: 0},
            name="rows_back",
        )(
            source, tie(taps, *waits), d_partial, d_partial, d_near, d_other, d_mixed, out_grad,
            *([] if before is None else [before]),
        )

    for n, later in enumerate(phases[1:]):
        takes = [send(small) for send in exchanges(later)]
        if n == 0:
            image_grad = rows_back(0, None, small)
        small = sum([tie(take, image_grad) for take in takes], small)

    def last_rows(sent):
        found.append(rows_back(1, image_grad, *sent))
        return found[-1:]

    weights = gather(tie(weights, small), phases[0], last_rows)
    image_grad = found[-1]
    cut = hidden // 4
    half_block = pl.BlockSpec((chans, cut), lambda k: (0, k))
    d_win, d_wout = pl.pallas_call(
        finish_kernel,
        grid=(4,),
        in_specs=[SCALARS, half_block, half_block],
        out_specs=[half_block, pl.BlockSpec((cut, chans), lambda k: (k, 0))],
        out_shape=[
            jax.ShapeDtypeStruct((chans, hidden), F32),
            jax.ShapeDtypeStruct((hidden, chans), F32),
        ],
        compiler_params=params(16),
        cost_estimate=cost(3),
        name="weight_grads",
    )(place_in([core])[None], weights, swap(weights, *core))
    vector = jax.ShapeDtypeStruct((chans,), F32)
    g_rate, g_freq, g_re, g_im, g_step, d_bin, d_skip, d_gain, d_bias, d_bout, d_scale = pl.pallas_call(
        taps_grad_kernel,
        out_shape=[mode_shape] * 4
        + [jax.ShapeDtypeStruct((2, chans), F32), jax.ShapeDtypeStruct((hidden,), F32)]
        + [vector] * 5,
        cost_estimate=cost(3),
        name="taps_grad",
    )(zr, zi, cr_t, ci_t, rate_t, freq_t, log_step, small)
    g_rate, g_freq, g_re, g_im = (v.transpose(0, 2, 1) for v in (g_rate, g_freq, g_re, g_im))
    return (
        output, image_grad, g_rate, g_freq, g_re, g_im, g_step, d_skip, d_gain, d_bias,
        d_win, d_bin, d_wout, d_bout, d_scale,
    )


def solution(mesh):
    tiled = P("th", "tw", None)
    return jax.shard_map(
        per_device,
        mesh=mesh,
        in_specs=(tiled,) + (P(),) * 14 + (tiled,),
        out_specs=(tiled, tiled) + (P(),) * 13,
        check_vma=False,
    )
```
